128 devices in a mesh: gx: 8 (over x, z_hi), gy: 4 (over y), gz: 4 (over z_lo, core).
Axes of the slice: x: 4, y: 4, z: 4 (z_hi: 2, z_lo: 2; z = z_hi * 2 + z_lo), core: 2. Of those that a mesh axis runs over, the one named last changes fastest.
Arguments:
- pre_act: bfloat16 [2048, 24576], P('gx', ('gy', 'gz')), may hold values from -6 to 6
- grad_out: bfloat16 [2048, 6144], P(('gx', 'gy'), 'gz'), may hold values from -0.3125 to 0.3125
- weight: bfloat16 [3072, 8, 6144], P('gy', 'gx', 'gz'), may hold values from -6 to 6
Outputs:
- pre_grad: bfloat16 [2048, 24576], P('gx', ('gy', 'gz'))
- weight_grad: bfloat16 [3072, 8, 6144], P('gy', 'gx', 'gz')
The draws below stay inside these ranges and needn't reach their ends.
All inputs are finite; a program needn't handle non-finite values.
Results may differ from the reference program's by a relative error of at most 0.02.
Values may be sent and summed in bfloat16 or wider, within the bound.
No kernel may reach another device: no remote copies, remote signals or barrier semaphores. Data moves between devices by JAX's collectives and lax.ppermute only.
A program may use at most 128 MiB of HBM per device.

```python
import jax
import jax.numpy as jnp
from jax import lax

DMODEL = 6144
FFN = 24576
TOK_DEV = 256
TOKENS = 2048
N_GX = 8
N_GZ = 4


def level_of(stream_key, shape, shards, least, high):
    def one(dim, shards_of):
        steps = jax.random.uniform(jax.random.fold_in(jax.random.fold_in(stream_key, 6), dim), (shards_of,), jnp.float32, least / len(shards), high / len(shards))
        return jnp.repeat(jnp.exp(steps), shape[dim] // shards_of).reshape((-1,) + (1,) * (len(shape) - dim - 1))

    factor_of = one(*shards[0])
    for cut in shards[1:]:
        factor_of = factor_of * one(*cut)
    return factor_of


def normal_values(own_key, dims, scale, reach, pieces=(), dtype=jnp.bfloat16):
    array = scale * jax.random.normal(own_key, dims, jnp.float32)
    if pieces:
        array = array * level_of(own_key, dims, pieces, -0.22, 0.18)
    return jnp.clip(array, -reach, reach).astype(dtype)


def setup_inputs(seed: int = 0) -> dict:
    seeds = jax.random.split(jax.random.key(seed), 4)
    return {
        "pre_act": normal_values(seeds[0], (TOKENS, FFN), 1.0, 6.0, ((0, 8), (1, 16))),
        "grad_out": normal_values(seeds[1], (TOKENS, DMODEL), (TOKENS ** -0.5), 0.3125, ((0, 32), (1, 4))),
        "weight": normal_values(seeds[2], (FFN // N_GX, N_GX, DMODEL), (TOKENS ** 0.5 * DMODEL ** -0.5), 6.0, ((0, 4), (1, 8), (2, 4))),
    }


tanh_scale = 0.7978845608028654
cubic_coef = 0.044715


def gelu_parts(inputs):
    inner = tanh_scale * (inputs + cubic_coef * inputs * inputs * inputs)
    tangent = jnp.tanh(inner)
    gelu_value = 0.5 * inputs * (1.0 + tangent)
    gelu_slope = 0.5 * (1.0 + tangent) + 0.5 * inputs * (1.0 - tangent * tangent) * tanh_scale * (1.0 + 3.0 * cubic_coef * inputs * inputs)
    return gelu_value, gelu_slope


def reference(pre_act, grad_out, weight):
    weight_flat = weight.reshape(FFN, DMODEL)
    gelu_value, gelu_slope = gelu_parts(pre_act.astype(jnp.float32))
    hidden = gelu_value.astype(jnp.bfloat16)
    width_block = DMODEL // N_GZ

    def add_width(block_index, running):
        offset = jnp.asarray(block_index, jnp.int32) * width_block
        grad_cols = lax.dynamic_slice_in_dim(grad_out, offset, width_block, 1)
        weight_cols = lax.dynamic_slice_in_dim(weight_flat, offset, width_block, 1)
        partial_block = lax.dot_general(grad_cols, weight_cols, (((1,), (1,)), ((), ())), preferred_element_type=jnp.float32)
        partial_block = lax.optimization_barrier(partial_block.astype(jnp.bfloat16))
        return running + partial_block.astype(jnp.float32)

    summed = lax.fori_loop(0, N_GZ, add_width, jnp.zeros((TOKENS, FFN), jnp.float32))
    pre_grad = (summed * gelu_slope).astype(jnp.bfloat16)

    def add_tokens(block_index, running):
        offset = jnp.asarray(block_index, jnp.int32) * TOK_DEV
        hidden_rows = lax.dynamic_slice_in_dim(hidden, offset, TOK_DEV, 0)
        grad_rows = lax.dynamic_slice_in_dim(grad_out, offset, TOK_DEV, 0)
        partial_block = lax.dot_general(hidden_rows, grad_rows, (((0,), (0,)), ((), ())), preferred_element_type=jnp.float32)
        partial_block = lax.optimization_barrier(partial_block.astype(jnp.bfloat16))
        return running + partial_block.astype(jnp.float32)

    weight_sum = lax.fori_loop(0, N_GX, add_tokens, jnp.zeros((FFN, DMODEL), jnp.float32))
    weight_grad = weight_sum.astype(jnp.bfloat16).reshape(FFN // N_GX, N_GX, DMODEL)
    return pre_grad, weight_grad
```

```python
import jax
import jax.numpy as jnp
from jax import lax
from jax.sharding import PartitionSpec as P

tanh_scale = 0.7978845608028654
cubic_coef = 0.044715


def gelu_value(u):
    t = jnp.tanh(tanh_scale * (u + cubic_coef * u * u * u))
    return 0.5 * u * (1.0 + t)


def gelu_slope(u):
    t = jnp.tanh(tanh_scale * (u + cubic_coef * u * u * u))
    return 0.5 * (1.0 + t) + 0.5 * u * (1.0 - t * t) * tanh_scale * (1.0 + 3.0 * cubic_coef * u * u)


def per_device(pre_act, grad_out, weight):
    groups = lax.axis_size("gx")
    tokens, columns = pre_act.shape
    rows = columns // groups
    grad_all = lax.all_gather(grad_out, ("gx", "gy"), axis=0, tiled=True)
    split = pre_act.reshape(tokens, rows, groups).transpose(2, 0, 1)
    mine = lax.all_to_all(split, "gx", split_axis=0, concat_axis=0, tiled=True)
    mine = mine.reshape(groups * tokens, rows)
    own = lax.all_gather(mine, "gz", axis=1, tiled=True)
    hidden = gelu_value(own.astype(jnp.float32)).astype(jnp.bfloat16)
    w = weight.reshape(weight.shape[0], weight.shape[2])
    part = jnp.einsum("td,rd->tr", grad_all, w, preferred_element_type=jnp.float32).astype(jnp.bfloat16)
    summed = lax.psum_scatter(part, "gz", scatter_dimension=1, tiled=True)
    back = lax.all_to_all(
        summed.reshape(groups, tokens, rows), "gx", split_axis=0, concat_axis=0, tiled=True
    )
    back = back.transpose(1, 2, 0).reshape(tokens, columns)
    pre_grad = (back.astype(jnp.float32) * gelu_slope(pre_act.astype(jnp.float32))).astype(jnp.bfloat16)
    weight_grad = jnp.einsum(
        "tr,td->rd", hidden, grad_all, preferred_element_type=jnp.float32
    ).astype(jnp.bfloat16)
    return pre_grad, weight_grad.reshape(weight.shape)


def solution(mesh):
    placed = (P("gx", ("gy", "gz")), P(("gx", "gy"), "gz"), P("gy", "gx", "gz"))
    return jax.shard_map(
        per_device,
        mesh=mesh,
        in_specs=placed,
        out_specs=(P("gx", ("gy", "gz")), P("gy", "gx", "gz")),
        check_vma=False,
    )
```

```python
import jax
import jax.numpy as jnp
from jax import lax
from jax.sharding import PartitionSpec as P

tanh_scale = 0.7978845608028654
cubic_coef = 0.044715
bf16 = jnp.bfloat16
f32 = jnp.float32


def gelu_value(u):
    t = jnp.tanh(tanh_scale * (u + cubic_coef * u * u * u))
    return 0.5 * u * (1.0 + t)


def gelu_slope(u):
    t = jnp.tanh(tanh_scale * (u + cubic_coef * u * u * u))
    return 0.5 * (1.0 + t) + 0.5 * u * (1.0 - t * t) * tanh_scale * (1.0 + 3.0 * cubic_coef * u * u)


def send(v, axis, count, to):
    return lax.ppermute(v, axis, [(i, to(i)) for i in range(count)])


def send_x(v, d):
    return send(v, "gx", 8, lambda i: ((i // 2 + d) % 4) * 2 + i % 2)


def send_y(v, d):
    return send(v, "gy", 4, lambda i: (i + d) % 4)


def swap_z_hi(v):
    return send(v, "gx", 8, lambda i: i ^ 1)


def swap_z_lo(v):
    return send(v, "gz", 4, lambda i: i ^ 2)


def swap_core(v):
    return send(v, "gz", 4, lambda i: i ^ 1)


def mirror(v, axis, at):
    n = v.shape[axis]
    twice = jnp.flip(jnp.concatenate([v, v], axis), axis)
    return lax.dynamic_slice_in_dim(twice, n - 1 - at, n, axis)


def gather_grad(grad_out):
    half = grad_out.shape[0] // 2
    other = swap_z_hi(grad_out)
    a = jnp.stack([grad_out[:half], other[:half]])
    b = jnp.stack([grad_out[half:], other[half:]])
    a4 = jnp.stack([a] + [send_y(a, k) for k in (1, 2, 3)], 1)
    b4 = jnp.stack([b] + [send_x(b, k) for k in (1, 2, 3)], 0)
    a1, a3 = send_x(a4, 1), send_x(a4, 3)
    b1, b3 = send_y(b4, 1), send_y(b4, 3)
    a2 = jnp.concatenate([send_x(a1[:1], 1), send_x(a3[1:], 3)], 0)
    b2 = jnp.concatenate([send_y(b1[:2], 1), send_y(b3[2:], 3)], 0)
    in_a = jnp.stack([a4, a1, a2, a3])
    in_b = jnp.stack([b4, b1, b2, b3], 2)
    return jnp.stack([in_a, in_b], 2)


def per_device(pre_act, grad_out, weight):
    tokens, columns = pre_act.shape
    rows = columns // 8
    gx, y, gz = lax.axis_index("gx"), lax.axis_index("gy"), lax.axis_index("gz")
    x, z_hi, z_lo, core = gx // 2, gx % 2, gz // 2, gz % 2
    w = weight.reshape(weight.shape[0], weight.shape[2])

    ordered = mirror(pre_act.reshape(4, 2, tokens // 8, columns), 0, y).transpose(1, 0, 2, 3)
    split = ordered.reshape(tokens, rows, 8).transpose(2, 1, 0)
    split = mirror(mirror(split.reshape(4, 2, rows, tokens), 0, x), 1, z_hi)
    from_z = jnp.stack([split[:, 0], swap_z_hi(split[:, 1])], 1)
    by_x = [from_z[0]] + [send_x(from_z[4 - k], k) for k in (1, 2, 3)]
    from_x = jnp.stack(by_x)
    pair = jnp.stack([from_x, swap_z_lo(from_x)])
    quad = jnp.stack([pair, swap_core(pair)], 1)
    quad = mirror(mirror(quad, 0, z_lo), 1, core)
    own = quad.transpose(0, 1, 4, 2, 3, 5).reshape(4 * rows, 8 * tokens)
    hidden = gelu_value(own.astype(f32)).astype(bf16)

    grad_all = gather_grad(grad_out).reshape(8 * tokens, -1)

    part = jnp.einsum("rd,td->rt", w, grad_all, preferred_element_type=f32).astype(bf16)
    part = mirror(part.reshape(2, 2, rows, 8 * tokens), 1, core)
    pair_sum = (part[:, 0].astype(f32) + swap_core(part[:, 1]).astype(f32)).astype(bf16)
    away = pair_sum.reshape(2, rows, 4, 2, tokens).transpose(2, 3, 0, 1, 4)
    away = mirror(mirror(away, 0, x), 1, z_hi)
    groups = [[2 * (2 * i + k) + c for i in range(8) for k in range(2)] for c in range(2)]
    back = lax.all_to_all(
        away.reshape(16, rows, tokens), ("gx", "gz"), 0, 0, tiled=True, axis_index_groups=groups
    ).reshape(8, 2, rows, tokens)
    back = back[:, 0].astype(f32) + back[:, 1].astype(f32)
    back = back.astype(bf16).transpose(2, 1, 0).reshape(2, 4, tokens // 8, columns)
    back = mirror(back.transpose(1, 0, 2, 3), 0, y).reshape(tokens, columns)
    pre_grad = (back.astype(f32) * gelu_slope(pre_act.astype(f32))).astype(bf16)

    weight_grad = jnp.einsum("rt,td->rd", hidden, grad_all, preferred_element_type=f32)
    return pre_grad, weight_grad.astype(bf16).reshape(weight.shape)


def solution(mesh):
    placed = (P("gx", ("gy", "gz")), P(("gx", "gy"), "gz"), P("gy", "gx", "gz"))
    return jax.shard_map(
        per_device,
        mesh=mesh,
        in_specs=placed,
        out_specs=(P("gx", ("gy", "gz")), P("gy", "gx", "gz")),
        check_vma=False,
    )
```

```python
import functools

import jax
import jax.numpy as jnp
from jax import lax
from jax.experimental import pallas as pl
from jax.experimental.pallas import tpu as pltpu
from jax.sharding import PartitionSpec as P

tanh_scale = 0.7978845608028654
cubic_coef = 0.044715
bf16 = jnp.bfloat16
f32 = jnp.float32
MIB = 1024 * 1024
VMEM = pl.BlockSpec(memory_space=pltpu.VMEM)
SMEM = pl.BlockSpec(memory_space=pltpu.SMEM)
ANY = pl.BlockSpec(memory_space=pl.ANY)


def send(v, axis, count, to):
    return lax.ppermute(v, axis, [(i, to(i)) for i in range(count)])


def send_x(v, d):
    return send(v, "gx", 8, lambda i: ((i // 2 + d) % 4) * 2 + i % 2)


def send_y(v, d):
    return send(v, "gy", 4, lambda i: (i + d) % 4)


def swap_z_hi(v):
    return send(v, "gx", 8, lambda i: i ^ 1)


def swap_z_lo(v):
    return send(v, "gz", 4, lambda i: i ^ 2)


def swap_core(v):
    return send(v, "gz", 4, lambda i: i ^ 1)


def call(body, out_shape, in_specs, cost, out_specs=None, scratch=(), limit=56):
    if out_specs is None:
        out_specs = [VMEM] * len(out_shape)
    flops, moved = cost
    return pl.pallas_call(
        body,
        out_shape=[jax.ShapeDtypeStruct(*s) for s in out_shape],
        in_specs=in_specs,
        out_specs=out_specs,
        scratch_shapes=list(scratch),
        compiler_params=pltpu.CompilerParams(vmem_limit_bytes=limit * MIB),
        cost_estimate=pl.CostEstimate(flops=flops, bytes_accessed=moved, transcendentals=0),
    )


def one_hot(at, rows):
    q = lax.broadcasted_iota(jnp.int32, (rows, 256), 0)
    u = lax.broadcasted_iota(jnp.int32, (rows, 256), 1)
    i, r = q // 32, q % 32
    s = ((at[0] - i // 2) & 3) * 2 + ((at[1] + i) & 1)
    return jnp.where(u == r * 8 + s, 1.0, 0.0).astype(bf16)


def token_rows(y, half, k):
    return pl.ds(pl.multiple_of(((y - k) & 3) * 64 + half * 32, 32), 32)


def pack_body(at, pre, *outs):
    slope, parts = outs[0], outs[1:]
    pick = one_hot(at, 256)
    for j in range(pre.shape[1] // 256):
        cols = slice(256 * j, 256 * j + 256)
        u = jnp.concatenate([pre[token_rows(at[2], h, k), cols] for h in range(2) for k in range(4)], 0)
        u = u.astype(f32)
        t = jnp.tanh(tanh_scale * (u + cubic_coef * u * u * u))
        slope[:, cols] = 0.5 * (1.0 + t) + 0.5 * u * (1.0 - t * t) * tanh_scale * (
            1.0 + 3.0 * cubic_coef * u * u
        )
        hidden = (0.5 * u * (1.0 + t)).astype(bf16)
        turned = lax.dot_general(pick, hidden, (((1,), (1,)), ((), ())), preferred_element_type=f32)
        turned = turned.astype(bf16)
        for i in range(8):
            parts[i][32 * j : 32 * j + 32, :] = turned[32 * i : 32 * i + 32, :]


def grad_copies(pieces, held, sems):
    a4, a1, a3, a2p, a2m, b4, b1, b3, b2p, b2m = pieces
    lower, todo = pl.ds(0, 128), []
    for k, src in ((0, a4), (1, a1), (3, a3)):
        todo.append((src, held.at[k, :, lower, :]))
    todo.append((a2p, held.at[2, pl.ds(0, 1), lower, :]))
    todo.append((a2m, held.at[2, pl.ds(1, 1), lower, :]))
    for k, src in ((0, b4), (1, b1), (3, b3)):
        todo.append((src, held.at[:, :, pl.ds(128 + 32 * k, 32), :]))
    todo.append((b2p, held.at[pl.ds(0, 2), :, pl.ds(192, 32), :]))
    todo.append((b2m, held.at[pl.ds(2, 2), :, pl.ds(192, 32), :]))
    return [pltpu.make_async_copy(s, d, sems.at[n]) for n, (s, d) in enumerate(todo)]


def input_body(at, w, *refs):
    pieces, (mine, theirs, held, sems) = refs[:10], refs[10:]
    copies = grad_copies(pieces, held, sems)
    for c in copies:
        c.start()
    for c in copies:
        c.wait()
    rows = w.shape[0] // 4
    ws = []
    for core, out in ((0, mine), (1, theirs)):
        for lo in range(2):
            block = ((at[3] + lo) & 1) * 2 + ((at[4] + core) & 1)
            ws.append(w[pl.ds(pl.multiple_of(block * rows, 64), rows), :])
    turned = jnp.concatenate(ws, 0)

    @pl.loop(0, 8)
    def _(d):
        k, z = d // 2, d % 2
        part = lax.dot_general(
            turned, held[k, z], (((1,), (1,)), ((), ())), preferred_element_type=f32
        ).astype(bf16)
        for lo in range(2):
            mine[lo, z, k] = part[lo * rows : lo * rows + rows]
            theirs[lo, z, k] = part[(lo + 2) * rows : (lo + 3) * rows]


def core_sum_body(mine, other, *outs):
    for lo in range(2):
        for z in range(2):
            for k in range(4):
                total = mine[lo, z, k].astype(f32) + other[lo, z, k].astype(f32)
                outs[lo * 2 + z][k] = total.astype(bf16)


def z_sum_body(r00, r01, r10, r11, *outs):
    for k in range(4):
        outs[k][0] = (r00[k].astype(f32) + r10[k].astype(f32)).astype(bf16)
        outs[k][1] = (r01[k].astype(f32) + r11[k].astype(f32)).astype(bf16)


def finish_body(at, slope, p0, p1, p2, p3, out):
    pick = one_hot(at, 256)
    for j in range(out.shape[1] // 256):
        cols = slice(256 * j, 256 * j + 256)
        v = jnp.concatenate([p[z, 32 * j : 32 * j + 32, :] for p in (p0, p1, p2, p3) for z in range(2)], 0)
        total = lax.dot_general(v, pick, (((0,), (0,)), ((), ())), preferred_element_type=f32)
        result = (total * slope[:, cols]).astype(bf16)
        for h in range(2):
            for k in range(4):
                n = (h * 4 + k) * 32
                out[token_rows(at[2], h, k), cols] = result[n : n + 32, :]


def weight_body(at, *refs):
    hidden, pieces, (out, held, sems) = refs[:4], refs[4:14], refs[14:]
    copies = grad_copies(pieces, held, sems)
    for c in copies:
        c.start()
    for c in copies:
        c.wait()
    rows = out.shape[0] // 4
    lhs = jnp.concatenate(
        [jnp.concatenate([h[d] for d in range(8)], 1) for h in hidden], 0
    )

    @pl.loop(0, out.shape[1] // 256)
    def _(j):
        cols = pl.ds(pl.multiple_of(j * 256, 256), 256)
        grads = held[:, :, :, cols].reshape(2048, 256)
        total = lax.dot_general(lhs, grads, (((1,), (0,)), ((), ())), preferred_element_type=f32)
        total = total.astype(bf16)
        for n, (lo, core) in enumerate(((0, 0), (1, 0), (0, 1), (1, 1))):
            block = ((at[3] + lo) & 1) * 2 + ((at[4] + core) & 1)
            out[pl.ds(pl.multiple_of(block * rows, 64), rows), cols] = total[n * rows : n * rows + rows]


def gather_grad(grad_out):
    half = grad_out.shape[0] // 2
    other = swap_z_hi(grad_out)
    a = jnp.stack([grad_out[:half], other[:half]])
    b = jnp.stack([grad_out[half:], other[half:]])
    a4 = jnp.stack([a] + [send_y(a, k) for k in (1, 2, 3)], 1)
    b4 = jnp.stack([b] + [send_x(b, k) for k in (1, 2, 3)], 0)
    a1, a3 = send_x(a4, 1), send_x(a4, 3)
    b1, b3 = send_y(b4, 1), send_y(b4, 3)
    a2p, a2m = send_x(a1[:1], 1), send_x(a3[1:], 3)
    b2p, b2m = send_y(b1[:2], 1), send_y(b3[2:], 3)
    a = [v.reshape(-1, 4 * half, v.shape[-1]) for v in (a4, a1, a3, a2p, a2m)]
    return a + [b4, b1, b3, b2p, b2m]


def per_device(pre_act, grad_out, weight):
    tokens, columns = pre_act.shape
    rows, features = columns // 8, grad_out.shape[1]
    gx, y, gz = lax.axis_index("gx"), lax.axis_index("gy"), lax.axis_index("gz")
    at = jnp.stack([gx // 2, gx % 2, y, gz // 2, gz % 2]).astype(jnp.int32)
    w = weight.reshape(4 * rows, features)
    block = (rows, tokens)
    grad_scratch = [pltpu.VMEM((4, 2, tokens, features), bf16), pltpu.SemaphoreType.DMA((10,))]
    product = 2 * 4 * rows * 8 * tokens * features

    slope, *parts = call(
        pack_body,
        [((tokens, columns), f32)] + [(block, bf16)] * 8,
        [SMEM, VMEM],
        (2 * tokens * 256 * columns, 8 * tokens * columns),
    )(at, pre_act)

    pieces = gather_grad(grad_out)

    got = [None] * 8
    for k in range(4):
        for z in range(2):
            to = lambda i, k=k, z=z: ((i // 2 - k) % 4) * 2 + (i % 2 ^ z)
            moved = parts[2 * k + z] if k == z == 0 else send(parts[2 * k + z], "gx", 8, to)
            got[2 * ((4 - k) % 4) + z] = moved
    own = jnp.stack(got)
    far = swap_z_lo(own)
    hidden = [own, far, swap_core(own), swap_core(far)]

    shape = ((2, 2, 4) + block, bf16)
    mine, theirs = call(
        input_body,
        [shape, shape],
        [SMEM, VMEM] + [ANY] * 10,
        (product, 2 * (6 * rows * features + 2048 * features)),
        scratch=grad_scratch,
    )(at, w, *pieces)
    other = swap_core(theirs)
    size = 2 * 4 * rows * tokens
    r00, r01, r10, r11 = call(
        core_sum_body, [((4,) + block, bf16)] * 4, [VMEM] * 2, (4 * size, 12 * size)
    )(mine, other)
    q01, q10 = swap_z_hi(r01), swap_z_lo(r10)
    q11 = send(r11, ("gx", "gz"), 32, lambda i: i ^ 6)
    sums = call(z_sum_body, [((2,) + block, bf16)] * 4, [VMEM] * 4, (2 * size, 6 * size))(
        r00, q01, q10, q11
    )
    back = [sums[0]] + [send_x(sums[4 - k], k) for k in (1, 2, 3)]
    (pre_grad,) = call(
        finish_body,
        [((tokens, columns), bf16)],
        [SMEM] + [VMEM] * 5,
        (2 * tokens * 256 * columns, 8 * tokens * columns),
    )(at, slope, *back)
    (weight_grad,) = call(
        weight_body,
        [((4 * rows, features), bf16)],
        [SMEM] + [VMEM] * 4 + [ANY] * 10,
        (product, 2 * (8 * rows * features + 2048 * features)),
        scratch=grad_scratch,
    )(at, *hidden, *pieces)
    return pre_grad, weight_grad.reshape(weight.shape)


def solution(mesh):
    placed = (P("gx", ("gy", "gz")), P(("gx", "gy"), "gz"), P("gy", "gx", "gz"))
    return jax.shard_map(
        per_device,
        mesh=mesh,
        in_specs=placed,
        out_specs=(P("gx", ("gy", "gz")), P("gy", "gx", "gz")),
        check_vma=False,
    )
```

```python
import functools

import jax
import jax.numpy as jnp
from jax import lax
from jax.experimental import pallas as pl
from jax.experimental.pallas import tpu as pltpu
from jax.sharding import PartitionSpec as P

tanh_scale = 0.7978845608028654
cubic_coef = 0.044715
bf16 = jnp.bfloat16
f32 = jnp.float32
MIB = 1024 * 1024
VMEM = pl.BlockSpec(memory_space=pltpu.VMEM)
SMEM = pl.BlockSpec(memory_space=pltpu.SMEM)
ANY = pl.BlockSpec(memory_space=pl.ANY)


def send(v, axis, count, to):
    return lax.ppermute(v, axis, [(i, to(i)) for i in range(count)])


def send_x(v, d):
    return send(v, "gx", 8, lambda i: ((i // 2 + d) % 4) * 2 + i % 2)


def send_y(v, d):
    return send(v, "gy", 4, lambda i: (i + d) % 4)


def swap_z_hi(v):
    return send(v, "gx", 8, lambda i: i ^ 1)


def swap_z_lo(v):
    return send(v, "gz", 4, lambda i: i ^ 2)


def swap_core(v):
    return send(v, "gz", 4, lambda i: i ^ 1)


def send_by_core(v, d, first):
    pairs = []
    for i in range(128):
        x, z_hi, y, z_lo, core = i // 32, i // 16 % 2, i // 4 % 4, i // 2 % 2, i % 2
        if (core == 0) == first:
            y = (y + d) % 4
        else:
            x = (x + d) % 4
        pairs.append((i, (((x * 2 + z_hi) * 4 + y) * 2 + z_lo) * 2 + core))
    return lax.ppermute(v, ("gx", "gy", "gz"), pairs)


def call(body, out_shape, in_specs, cost, out_specs=None, scratch=(), limit=56):
    if out_specs is None:
        out_specs = [VMEM] * len(out_shape)
    flops, moved = cost
    return pl.pallas_call(
        body,
        out_shape=[jax.ShapeDtypeStruct(*s) for s in out_shape],
        in_specs=in_specs,
        out_specs=out_specs,
        scratch_shapes=list(scratch),
        compiler_params=pltpu.CompilerParams(vmem_limit_bytes=limit * MIB),
        cost_estimate=pl.CostEstimate(flops=flops, bytes_accessed=moved, transcendentals=0),
    )


def one_hot(at, rows):
    q = lax.broadcasted_iota(jnp.int32, (rows, 256), 0)
    u = lax.broadcasted_iota(jnp.int32, (rows, 256), 1)
    i, r = q // 32, q % 32
    s = ((at[0] - i // 2) & 3) * 2 + ((at[1] + i) & 1)
    return jnp.where(u == r * 8 + s, 1.0, 0.0).astype(bf16)


def token_rows(y, k):
    return pl.ds(pl.multiple_of(((y - k) & 3) * 64, 64), 64)


def pack_body(at, pre, *outs):
    slope, parts = outs[0], outs[1:]
    pick = one_hot(at, 256)
    for j in range(pre.shape[1] // 256):
        cols = slice(256 * j, 256 * j + 256)
        u = jnp.concatenate([pre[token_rows(at[2], k), cols] for k in range(4)], 0)
        u = u.astype(f32)
        t = jnp.tanh(tanh_scale * (u + cubic_coef * u * u * u))
        slope[:, cols] = 0.5 * (1.0 + t) + 0.5 * u * (1.0 - t * t) * tanh_scale * (
            1.0 + 3.0 * cubic_coef * u * u
        )
        hidden = (0.5 * u * (1.0 + t)).astype(bf16)
        turned = lax.dot_general(pick, hidden, (((1,), (1,)), ((), ())), preferred_element_type=f32)
        turned = turned.astype(bf16)
        for i in range(8):
            parts[i // 2][i % 2, 32 * j : 32 * j + 32, :] = turned[32 * i : 32 * i + 32, :]


def load_grads(at, pieces, held, sems):
    p0, p1, p3, p2p, p2m = pieces
    todo = [(p0, 0, 0), (p0, 0, 1), (p1, 1, 0), (p1, 1, 1), (p3, 3, 0), (p3, 3, 1), (p2p, 2, 0), (p2m, 2, 1)]

    def copies(core):
        made = []
        for n, (src, k, z) in enumerate(todo):
            src = src.at[z if src.shape[0] == 2 else 0]
            dst = held.at[k, z] if core == 0 else held.at[:, z, k]
            made.append(pltpu.make_async_copy(src, dst, sems.at[n]))
        return made

    for core in range(2):

        @pl.when(at[4] == core)
        def _():
            for c in copies(core):
                c.start()
            for c in copies(core):
                c.wait()


def input_body(at, w, *refs):
    pieces, (mine, theirs, held, sems) = refs[:5], refs[5:]
    load_grads(at, pieces, held, sems)
    rows = w.shape[0] // 4
    ws = []
    for core, out in ((0, mine), (1, theirs)):
        for lo in range(2):
            block = ((at[3] + lo) & 1) * 2 + ((at[4] + core) & 1)
            ws.append(w[pl.ds(pl.multiple_of(block * rows, 64), rows), :])
    turned = jnp.concatenate(ws, 0)

    @pl.loop(0, 8)
    def _(d):
        k, z = d // 2, d % 2
        part = lax.dot_general(
            turned, held[k, z].reshape(256, -1), (((1,), (1,)), ((), ())), preferred_element_type=f32
        ).astype(bf16)
        for lo in range(2):
            mine[lo, z, k] = part[lo * rows : lo * rows + rows]
            theirs[lo, z, k] = part[(lo + 2) * rows : (lo + 3) * rows]


def core_sum_body(mine, other, *outs):
    for lo in range(2):
        for z in range(2):
            for k in range(4):
                total = mine[lo, z, k].astype(f32) + other[lo, z, k].astype(f32)
                outs[lo * 2 + z][k] = total.astype(bf16)


def z_sum_body(r00, r01, r10, r11, *outs):
    for k in range(4):
        outs[k][0] = (r00[k].astype(f32) + r10[k].astype(f32)).astype(bf16)
        outs[k][1] = (r01[k].astype(f32) + r11[k].astype(f32)).astype(bf16)


def finish_body(at, slope, p0, p1, p2, p3, out):
    pick = one_hot(at, 256)
    for j in range(out.shape[1] // 256):
        cols = slice(256 * j, 256 * j + 256)
        v = jnp.concatenate([p[z, 32 * j : 32 * j + 32, :] for p in (p0, p1, p2, p3) for z in range(2)], 0)
        total = lax.dot_general(v, pick, (((0,), (0,)), ((), ())), preferred_element_type=f32)
        result = (total * slope[:, cols]).astype(bf16)
        for k in range(4):
            out[token_rows(at[2], k), cols] = result[64 * k : 64 * k + 64, :]


def weight_body(at, *refs):
    hidden, pieces, (out, held, sems) = refs[:4], refs[4:9], refs[9:]
    load_grads(at, pieces, held, sems)
    rows = out.shape[0] // 4
    lhs = jnp.concatenate(
        [jnp.concatenate([h[z, k] for k in range(4) for z in range(2)], 1) for h in hidden], 0
    )

    @pl.loop(0, out.shape[1] // 256)
    def _(j):
        cols = pl.ds(pl.multiple_of(j * 256, 256), 256)
        grads = held[:, :, :, :, cols].reshape(2048, 256)
        total = lax.dot_general(lhs, grads, (((1,), (0,)), ((), ())), preferred_element_type=f32)
        total = total.astype(bf16)
        for n, (lo, core) in enumerate(((0, 0), (1, 0), (0, 1), (1, 1))):
            block = ((at[3] + lo) & 1) * 2 + ((at[4] + core) & 1)
            out[pl.ds(pl.multiple_of(block * rows, 64), rows), cols] = total[n * rows : n * rows + rows]


def gather_grad(grad_out, first):
    other, first = lax.optimization_barrier((swap_z_hi(grad_out), first))
    both = jnp.stack([grad_out, other])
    p0 = jnp.stack([both] + [send_by_core(both, k, True) for k in (1, 2, 3)], 1)
    p1, p3 = send_by_core(p0, 1, False), send_by_core(p0, 3, False)
    return (p0, p1, p3, send_by_core(p1[:1], 1, False), send_by_core(p3[1:], 3, False)), first


def per_device(pre_act, grad_out, weight):
    tokens, columns = pre_act.shape
    rows, features = columns // 8, grad_out.shape[1]
    gx, y, gz = lax.axis_index("gx"), lax.axis_index("gy"), lax.axis_index("gz")
    at = jnp.stack([gx // 2, gx % 2, y, gz // 2, gz % 2]).astype(jnp.int32)
    w = weight.reshape(4 * rows, features)
    block = (rows, tokens)
    grad_scratch = [pltpu.VMEM((4, 2, 4, tokens // 4, features), bf16), pltpu.SemaphoreType.DMA((8,))]
    product = 2 * 4 * rows * 8 * tokens * features

    slope, *parts = call(
        pack_body,
        [((tokens, columns), f32)] + [((2,) + block, bf16)] * 4,
        [SMEM, VMEM],
        (2 * tokens * 256 * columns, 8 * tokens * columns),
    )(at, pre_act)

    pieces, parts = gather_grad(grad_out, parts)

    by_x = [parts[0]] + [send_x(parts[4 - k], k) for k in (1, 2, 3)]
    by_x, _ = lax.optimization_barrier((by_x, pieces[0]))
    own = jnp.stack([p[0] for p in by_x])
    own = jnp.stack([own, swap_z_hi(jnp.stack([p[1] for p in by_x]))])
    own, _ = lax.optimization_barrier((own, pieces[1]))
    far = swap_z_lo(own)

    shape = ((2, 2, 4) + block, bf16)
    mine, theirs = call(
        input_body,
        [shape, shape],
        [SMEM, VMEM] + [ANY] * 5,
        (product, 2 * (6 * rows * features + 2048 * features)),
        scratch=grad_scratch,
    )(at, w, *pieces)
    other = swap_core(theirs)
    size = 2 * 4 * rows * tokens
    r00, r01, r10, r11 = call(
        core_sum_body, [((4,) + block, bf16)] * 4, [VMEM] * 2, (4 * size, 12 * size)
    )(mine, other)
    q01, q10 = swap_z_hi(r01), swap_z_lo(r10)
    q11 = send(r11, ("gx", "gz"), 32, lambda i: i ^ 6)
    own, far, _ = lax.optimization_barrier((own, far, r00))
    hidden = [own, far, swap_core(own), swap_core(far)]
    (weight_grad,) = call(
        weight_body,
        [((4 * rows, features), bf16)],
        [SMEM] + [VMEM] * 4 + [ANY] * 5,
        (product, 2 * (8 * rows * features + 2048 * features)),
        scratch=grad_scratch,
    )(at, *hidden, *pieces)
    q01, q10, q11, weight_grad = lax.optimization_barrier((q01, q10, q11, weight_grad))
    sums = call(z_sum_body, [((2,) + block, bf16)] * 4, [VMEM] * 4, (2 * size, 6 * size))(
        r00, q01, q10, q11
    )
    back = [sums[0]] + [send_x(sums[4 - k], k) for k in (1, 2, 3)]
    (pre_grad,) = call(
        finish_body,
        [((tokens, columns), bf16)],
        [SMEM] + [VMEM] * 5,
        (2 * tokens * 256 * columns, 8 * tokens * columns),
    )(at, slope, *back)
    return pre_grad, weight_grad.reshape(weight.shape)


def solution(mesh):
    placed = (P("gx", ("gy", "gz")), P(("gx", "gy"), "gz"), P("gy", "gx", "gz"))
    return jax.shard_map(
        per_device,
        mesh=mesh,
        in_specs=placed,
        out_specs=(P("gx", ("gy", "gz")), P("gy", "gx", "gz")),
        check_vma=False,
    )
```

```python
import functools

import jax
import jax.numpy as jnp
from jax import lax
from jax.experimental import pallas as pl
from jax.experimental.pallas import tpu as pltpu
from jax.sharding import PartitionSpec as P

tanh_scale = 0.7978845608028654
cubic_coef = 0.044715
bf16 = jnp.bfloat16
f32 = jnp.float32
MIB = 1024 * 1024
VMEM = pl.BlockSpec(memory_space=pltpu.VMEM)
SMEM = pl.BlockSpec(memory_space=pltpu.SMEM)
ANY = pl.BlockSpec(memory_space=pl.ANY)


def send(v, axis, count, to):
    return lax.ppermute(v, axis, [(i, to(i)) for i in range(count)])


def send_x(v, d):
    return send(v, "gx", 8, lambda i: ((i // 2 + d) % 4) * 2 + i % 2)


def send_y(v, d):
    return send(v, "gy", 4, lambda i: (i + d) % 4)


def swap_z_hi(v):
    return send(v, "gx", 8, lambda i: i ^ 1)


def swap_z_lo(v):
    return send(v, "gz", 4, lambda i: i ^ 2)


def swap_core(v):
    return send(v, "gz", 4, lambda i: i ^ 1)


def send_by_core(v, d, first):
    pairs = []
    for i in range(128):
        x, z_hi, y, z_lo, core = i // 32, i // 16 % 2, i // 4 % 4, i // 2 % 2, i % 2
        if (core == 0) == first:
            y = (y + d) % 4
        else:
            x = (x + d) % 4
        pairs.append((i, (((x * 2 + z_hi) * 4 + y) * 2 + z_lo) * 2 + core))
    return lax.ppermute(v, ("gx", "gy", "gz"), pairs)


def call(body, out_shape, in_specs, cost, out_specs=None, scratch=(), limit=56):
    if out_specs is None:
        out_specs = [VMEM] * len(out_shape)
    flops, moved = cost
    return pl.pallas_call(
        body,
        out_shape=[jax.ShapeDtypeStruct(*s) for s in out_shape],
        in_specs=in_specs,
        out_specs=out_specs,
        scratch_shapes=list(scratch),
        compiler_params=pltpu.CompilerParams(vmem_limit_bytes=limit * MIB),
        cost_estimate=pl.CostEstimate(flops=flops, bytes_accessed=moved, transcendentals=0),
    )


def one_hot(at, rows):
    q = lax.broadcasted_iota(jnp.int32, (rows, 256), 0)
    u = lax.broadcasted_iota(jnp.int32, (rows, 256), 1)
    i, r = q // 32, q % 32
    s = ((at[0] - i // 2) & 3) * 2 + ((at[1] + i) & 1)
    return jnp.where(u == r * 8 + s, 1.0, 0.0).astype(bf16)


def token_rows(y, k):
    return pl.ds(pl.multiple_of(((y - k) & 3) * 64, 64), 64)


def pack_body(at, pre, *outs):
    slope, parts = outs[0], outs[1:]
    pick = one_hot(at, 256)
    for j in range(pre.shape[1] // 256):
        cols = slice(256 * j, 256 * j + 256)
        u = jnp.concatenate([pre[token_rows(at[2], k), cols] for k in range(4)], 0)
        u = u.astype(f32)
        t = jnp.tanh(tanh_scale * (u + cubic_coef * u * u * u))
        slope[:, cols] = 0.5 * (1.0 + t) + 0.5 * u * (1.0 - t * t) * tanh_scale * (
            1.0 + 3.0 * cubic_coef * u * u
        )
        hidden = (0.5 * u * (1.0 + t)).astype(bf16)
        turned = lax.dot_general(pick, hidden, (((1,), (1,)), ((), ())), preferred_element_type=f32)
        turned = turned.astype(bf16)
        for i in range(8):
            parts[i][32 * j : 32 * j + 32, :] = turned[32 * i : 32 * i + 32, :]


def load_grads(at, pieces, held, sems):
    p0, p1, p3, p2p, p2m = pieces
    todo = [(p0, 0, 0), (p0, 0, 1), (p1, 1, 0), (p1, 1, 1), (p3, 3, 0), (p3, 3, 1), (p2p, 2, 0), (p2m, 2, 1)]

    def copies(core):
        made = []
        for n, (src, k, z) in enumerate(todo):
            src = src.at[z if src.shape[0] == 2 else 0]
            dst = held.at[k, z] if core == 0 else held.at[:, z, k]
            made.append(pltpu.make_async_copy(src, dst, sems.at[n]))
        return made

    for core in range(2):

        @pl.when(at[4] == core)
        def _():
            for c in copies(core):
                c.start()
            for c in copies(core):
                c.wait()


def input_body(count, at, w, *refs):
    pieces, (mine, theirs, held, sems) = refs[:count], refs[count:]
    blocks = [(n, z) for n, p in enumerate(pieces) for z in range(p.shape[0])]
    copies = [
        pltpu.make_async_copy(pieces[n].at[z], held.at[i], sems.at[i]) for i, (n, z) in enumerate(blocks)
    ]
    for c in copies:
        c.start()
    rows = w.shape[0] // 4
    for i, c in enumerate(copies):
        c.wait()
        part = lax.dot_general(
            w[...], held[i].reshape(256, -1), (((1,), (1,)), ((), ())), preferred_element_type=f32
        ).astype(bf16)
        for core in range(2):

            @pl.when(at[4] == core)
            def _():
                for n in range(4):
                    out = mine if n % 2 == core else theirs
                    out[i, at[3] ^ (n // 2)] = part[n * rows : n * rows + rows]


def core_sum_body(at, mine, mine2, other, other2, *outs):
    def block(early, late, k, z, lo):
        if k == 2:
            return late[z, lo]
        return early[2 * (k - k // 3) + z, lo]

    for core in range(2):

        @pl.when(at[4] == core)
        def _():
            by_x, by_y = (mine, mine2), (other, other2)
            if core:
                by_x, by_y = by_y, by_x
            for lo in range(2):
                for z in range(2):
                    y = [block(*by_y, k, z, lo) for k in range(4)]
                    for k in range(4):
                        turned = jnp.concatenate([v[:, 64 * k : 64 * k + 64] for v in y], 1)
                        total = block(*by_x, k, z, lo).astype(f32) + turned.astype(f32)
                        outs[lo * 2 + z][k] = total.astype(bf16)


def z_sum_body(r00, r01, r10, r11, *outs):
    for k in range(4):
        outs[k][0] = (r00[k].astype(f32) + r10[k].astype(f32)).astype(bf16)
        outs[k][1] = (r01[k].astype(f32) + r11[k].astype(f32)).astype(bf16)


def finish_body(at, slope, p0, p1, p2, p3, out):
    pick = one_hot(at, 256)
    for j in range(out.shape[1] // 256):
        cols = slice(256 * j, 256 * j + 256)
        v = jnp.concatenate([p[z, 32 * j : 32 * j + 32, :] for p in (p0, p1, p2, p3) for z in range(2)], 0)
        total = lax.dot_general(v, pick, (((0,), (0,)), ((), ())), preferred_element_type=f32)
        result = (total * slope[:, cols]).astype(bf16)
        for k in range(4):
            out[token_rows(at[2], k), cols] = result[64 * k : 64 * k + 64, :]


def weight_body(at, *refs):
    hidden, pieces, (out, held, sems) = refs[:4], refs[4:9], refs[9:]
    load_grads(at, pieces, held, sems)
    rows = out.shape[0] // 4
    lhs = jnp.concatenate(
        [jnp.concatenate([h[z, k] for k in range(4) for z in range(2)], 1) for h in hidden], 0
    )

    @pl.loop(0, out.shape[1] // 256)
    def _(j):
        cols = pl.ds(pl.multiple_of(j * 256, 256), 256)
        grads = held[:, :, :, :, cols].reshape(2048, 256)
        total = lax.dot_general(lhs, grads, (((1,), (0,)), ((), ())), preferred_element_type=f32)
        total = total.astype(bf16)
        for n, (lo, core) in enumerate(((0, 0), (1, 0), (0, 1), (1, 1))):
            block = ((at[3] + lo) & 1) * 2 + ((at[4] + core) & 1)
            out[pl.ds(pl.multiple_of(block * rows, 64), rows), cols] = total[n * rows : n * rows + rows]


def per_device(pre_act, grad_out, weight):
    tokens, columns = pre_act.shape
    rows, features = columns // 8, grad_out.shape[1]
    gx, y, gz = lax.axis_index("gx"), lax.axis_index("gy"), lax.axis_index("gz")
    at = jnp.stack([gx // 2, gx % 2, y, gz // 2, gz % 2]).astype(jnp.int32)
    w = weight.reshape(4 * rows, features)
    block = (rows, tokens)
    grad_scratch = [pltpu.VMEM((4, 2, 4, tokens // 4, features), bf16), pltpu.SemaphoreType.DMA((8,))]
    product = 2 * 4 * rows * 8 * tokens * features

    slope, *parts = call(
        pack_body,
        [((tokens, columns), f32)] + [(block, bf16)] * 8,
        [SMEM, VMEM],
        (2 * tokens * 256 * columns, 8 * tokens * columns),
    )(at, pre_act)

    other, parts = lax.optimization_barrier((swap_z_hi(grad_out), parts))
    both = jnp.stack([grad_out, other])
    p0 = jnp.stack([both] + [send_by_core(both, k, True) for k in (1, 2, 3)], 1)
    p0, parts = lax.optimization_barrier((p0, parts))
    p1, p3 = send_by_core(p0, 1, False), send_by_core(p0, 3, False)

    got = [None] * 8
    for k in range(4):
        for z in range(2):
            to = lambda i, k=k, z=z: ((i // 2 - k) % 4) * 2 + (i % 2 ^ z)
            moved = parts[2 * k + z] if k == z == 0 else send(parts[2 * k + z], "gx", 8, to)
            got[4 * z + (4 - k) % 4] = moved
    p1, p3, got = lax.optimization_barrier((p1, p3, got))
    p2p, p2m = send_by_core(p1[:1], 1, False), send_by_core(p3[1:], 3, False)
    pieces = p0, p1, p3, p2p, p2m
    own = jnp.stack(got).reshape((2, 4) + block)
    far = swap_z_lo(own)

    def input_part(*given):
        count = sum(p.shape[0] for p in given)
        return call(
            functools.partial(input_body, len(given)),
            [((count, 2) + block, bf16)] * 2,
            [SMEM, VMEM] + [ANY] * len(given),
            (product * count // 8, 2 * (4 * rows * features + count * (4 * rows + features) * tokens)),
            scratch=[
                pltpu.VMEM((count, 4, tokens // 4, features), bf16),
                pltpu.SemaphoreType.DMA((count,)),
            ],
        )(at, w, *given)

    mine, theirs = input_part(p0, p1, p3)
    other, p2p, p2m = lax.optimization_barrier((swap_core(theirs), p2p, p2m))
    mine2, theirs2 = input_part(p2p, p2m)
    size = 2 * 4 * rows * tokens
    r00, r01, r10, r11 = call(
        core_sum_body, [((4,) + block, bf16)] * 4, [SMEM] + [VMEM] * 4, (4 * size, 12 * size)
    )(at, mine, mine2, other, swap_core(theirs2))
    q01, q10 = swap_z_hi(r01), swap_z_lo(r10)
    q11 = send(r11, ("gx", "gz"), 32, lambda i: i ^ 6)
    own, far, _ = lax.optimization_barrier((own, far, r00))
    hidden = [own, far, swap_core(own), swap_core(far)]
    (weight_grad,) = call(
        weight_body,
        [((4 * rows, features), bf16)],
        [SMEM] + [VMEM] * 4 + [ANY] * 5,
        (product, 2 * (8 * rows * features + 2048 * features)),
        scratch=grad_scratch,
    )(at, *hidden, *pieces)
    q01, q10, q11, weight_grad = lax.optimization_barrier((q01, q10, q11, weight_grad))
    sums = call(z_sum_body, [((2,) + block, bf16)] * 4, [VMEM] * 4, (2 * size, 6 * size))(
        r00, q01, q10, q11
    )
    back = [sums[0]] + [send_x(sums[4 - k], k) for k in (1, 2, 3)]
    (pre_grad,) = call(
        finish_body,
        [((tokens, columns), bf16)],
        [SMEM] + [VMEM] * 5,
        (2 * tokens * 256 * columns, 8 * tokens * columns),
    )(at, slope, *back)
    return pre_grad, weight_grad.reshape(weight.shape)


def solution(mesh):
    placed = (P("gx", ("gy", "gz")), P(("gx", "gy"), "gz"), P("gy", "gx", "gz"))
    return jax.shard_map(
        per_device,
        mesh=mesh,
        in_specs=placed,
        out_specs=(P("gx", ("gy", "gz")), P("gy", "gx", "gz")),
        check_vma=False,
    )
```

```python
import functools

import jax
import jax.numpy as jnp
from jax import lax
from jax.experimental import pallas as pl
from jax.experimental.pallas import tpu as pltpu
from jax.sharding import PartitionSpec as P

tanh_scale = 0.7978845608028654
cubic_coef = 0.044715
bf16 = jnp.bfloat16
f32 = jnp.float32
MIB = 1024 * 1024
VMEM = pl.BlockSpec(memory_space=pltpu.VMEM)
SMEM = pl.BlockSpec(memory_space=pltpu.SMEM)
ANY = pl.BlockSpec(memory_space=pl.ANY)


def send(v, axis, count, to):
    return lax.ppermute(v, axis, [(i, to(i)) for i in range(count)])


def send_x(v, d):
    return send(v, "gx", 8, lambda i: ((i // 2 + d) % 4) * 2 + i % 2)


def send_y(v, d):
    return send(v, "gy", 4, lambda i: (i + d) % 4)


def swap_z_hi(v):
    return send(v, "gx", 8, lambda i: i ^ 1)


def swap_z_lo(v):
    return send(v, "gz", 4, lambda i: i ^ 2)


def swap_core(v):
    return send(v, "gz", 4, lambda i: i ^ 1)


def send_by_core(v, d, first):
    pairs = []
    for i in range(128):
        x, z_hi, y, z_lo, core = i // 32, i // 16 % 2, i // 4 % 4, i // 2 % 2, i % 2
        if (core == 0) == first:
            y = (y + d) % 4
        else:
            x = (x + d) % 4
        pairs.append((i, (((x * 2 + z_hi) * 4 + y) * 2 + z_lo) * 2 + core))
    return lax.ppermute(v, ("gx", "gy", "gz"), pairs)


def call(body, out_shape, in_specs, cost, out_specs=None, scratch=(), limit=56):
    if out_specs is None:
        out_specs = [VMEM] * len(out_shape)
    flops, moved = cost
    return pl.pallas_call(
        body,
        out_shape=[jax.ShapeDtypeStruct(*s) for s in out_shape],
        in_specs=in_specs,
        out_specs=out_specs,
        scratch_shapes=list(scratch),
        compiler_params=pltpu.CompilerParams(vmem_limit_bytes=limit * MIB),
        cost_estimate=pl.CostEstimate(flops=flops, bytes_accessed=moved, transcendentals=0),
    )


def one_hot():
    q = lax.broadcasted_iota(jnp.int32, (256, 256), 0)
    u = lax.broadcasted_iota(jnp.int32, (256, 256), 1)
    return jnp.where(u == (q % 32) * 8 + q // 32, 1.0, 0.0).astype(bf16)


def group(at, k, z):
    return ((at[0] - k) & 3) * 2 + (at[1] ^ z)


def token_rows(y, k):
    return pl.ds(pl.multiple_of(((y - k) & 3) * 64, 64), 64)


def pack_body(at, pre, *outs):
    slope, parts = outs
    pick = one_hot()
    for j in range(pre.shape[1] // 256):
        cols = slice(256 * j, 256 * j + 256)
        u = jnp.concatenate([pre[token_rows(at[2], k), cols] for k in range(4)], 0)
        u = u.astype(f32)
        t = jnp.tanh(tanh_scale * (u + cubic_coef * u * u * u))
        slope[:, cols] = 0.5 * (1.0 + t) + 0.5 * u * (1.0 - t * t) * tanh_scale * (
            1.0 + 3.0 * cubic_coef * u * u
        )
        hidden = (0.5 * u * (1.0 + t)).astype(bf16)
        turned = lax.dot_general(pick, hidden, (((1,), (1,)), ((), ())), preferred_element_type=f32)
        turned = turned.astype(bf16)
        for i in range(8):
            parts[i, 32 * j : 32 * j + 32, :] = turned[32 * i : 32 * i + 32, :]


def load_grads(at, pieces, held, sems):
    p0, p1, p3, p2p, p2m = pieces
    todo = [(p0, 0, 0), (p0, 0, 1), (p1, 1, 0), (p1, 1, 1), (p3, 3, 0), (p3, 3, 1), (p2p, 2, 0), (p2m, 2, 1)]

    def copies(core):
        made = []
        for n, (src, k, z) in enumerate(todo):
            src = src.at[z if src.shape[0] == 2 else 0]
            dst = held.at[k, z] if core == 0 else held.at[:, z, k]
            made.append(pltpu.make_async_copy(src, dst, sems.at[n]))
        return made

    for core in range(2):

        @pl.when(at[4] == core)
        def _():
            for c in copies(core):
                c.start()
            for c in copies(core):
                c.wait()


def input_body(count, at, w, *refs):
    pieces, (mine, theirs, held, sums, in_sems, out_sems) = refs[:count], refs[count:]
    blocks = [p.at[z] for p in pieces for z in range(p.shape[0])]
    for i, src in enumerate(blocks):
        pltpu.make_async_copy(src, held.at[i], in_sems.at[i]).start()
    rows = w.shape[0] // 4

    def leaving(i):
        slot = i % 2
        return [
            pltpu.make_async_copy(sums.at[slot, n], out.at[i], out_sems.at[slot, n])
            for n, out in enumerate((mine, theirs))
        ]

    @pl.loop(0, len(blocks))
    def _(i):
        pltpu.make_async_copy(blocks[0], held.at[i], in_sems.at[i]).wait()

        @pl.when(i >= 2)
        def _():
            for c in leaving(i - 2):
                c.wait()

        part = lax.dot_general(
            w[...], held[i].reshape(256, -1), (((1,), (1,)), ((), ())), preferred_element_type=f32
        ).astype(bf16)
        for n in range(4):
            sums[i % 2, at[4] ^ (n % 2), n // 2] = part[n * rows : n * rows + rows]
        for c in leaving(i):
            c.start()

    for i in range(len(blocks) - 2, len(blocks)):
        for c in leaving(i):
            c.wait()


def core_sum_body(at, mine, mine2, other, other2, out, held, sems):
    def leaving(k, z):
        n = 2 * k + z
        return pltpu.make_async_copy(held.at[n], out.at[group(at, k, z)], sems.at[n])

    def block(early, late, k, z, lo):
        if k == 2:
            return late[z, lo]
        return early[2 * (k - k // 3) + z, lo]

    for core in range(2):

        @pl.when(at[4] == core)
        def _():
            by_x, by_y = (mine, mine2), (other, other2)
            if core:
                by_x, by_y = by_y, by_x
            for z in range(2):
                for lo in range(2):
                    y = [block(*by_y, k, z, lo) for k in range(4)]
                    for k in range(4):
                        turned = jnp.concatenate([v[:, 64 * k : 64 * k + 64] for v in y], 1)
                        total = block(*by_x, k, z, lo).astype(f32) + turned.astype(f32)
                        held[2 * k + z, lo] = total.astype(bf16)
                for k in range(4):
                    leaving(k, z).start()

    for z in range(2):
        for k in range(4):
            leaving(k, z).wait()


def finish_body(at, slope, parts, out):
    pick = one_hot()
    for j in range(out.shape[1] // 256):
        cols, units = slice(256 * j, 256 * j + 256), slice(32 * j, 32 * j + 32)
        v = [(parts[n, 0, units, :].astype(f32) + parts[n, 1, units, :].astype(f32)) for n in range(8)]
        v = jnp.concatenate(v, 0).astype(bf16)
        total = lax.dot_general(v, pick, (((0,), (0,)), ((), ())), preferred_element_type=f32)
        result = (total * slope[:, cols]).astype(bf16)
        for k in range(4):
            out[token_rows(at[2], k), cols] = result[64 * k : 64 * k + 64, :]


def weight_body(at, *refs):
    hidden, pieces, (out, held, sems) = refs[:4], refs[4:9], refs[9:]
    load_grads(at, pieces, held, sems)
    rows = out.shape[0] // 4
    lhs = jnp.concatenate(
        [jnp.concatenate([h[group(at, k, z)] for k in range(4) for z in range(2)], 1) for h in hidden], 0
    )

    @pl.loop(0, out.shape[1] // 256)
    def _(j):
        cols = pl.ds(pl.multiple_of(j * 256, 256), 256)
        grads = held[:, :, :, :, cols].reshape(2048, 256)
        total = lax.dot_general(lhs, grads, (((1,), (0,)), ((), ())), preferred_element_type=f32)
        total = total.astype(bf16)
        for n, (lo, core) in enumerate(((0, 0), (1, 0), (0, 1), (1, 1))):
            block = ((at[3] + lo) & 1) * 2 + ((at[4] + core) & 1)
            out[pl.ds(pl.multiple_of(block * rows, 64), rows), cols] = total[n * rows : n * rows + rows]


def per_device(pre_act, grad_out, weight):
    tokens, columns = pre_act.shape
    rows, features = columns // 8, grad_out.shape[1]
    gx, y, gz = lax.axis_index("gx"), lax.axis_index("gy"), lax.axis_index("gz")
    at = jnp.stack([gx // 2, gx % 2, y, gz // 2, gz % 2]).astype(jnp.int32)
    w = weight.reshape(4 * rows, features)
    block = (rows, tokens)
    grad_scratch = [pltpu.VMEM((4, 2, 4, tokens // 4, features), bf16), pltpu.SemaphoreType.DMA((8,))]
    product = 2 * 4 * rows * 8 * tokens * features

    slope, parts = call(
        pack_body,
        [((tokens, columns), f32), ((8,) + block, bf16)],
        [SMEM, VMEM],
        (2 * tokens * 256 * columns, 8 * tokens * columns),
    )(at, pre_act)

    other, parts = lax.optimization_barrier((swap_z_hi(grad_out), parts))
    both = jnp.stack([grad_out, other])
    p0 = jnp.stack([both] + [send_by_core(both, k, True) for k in (1, 2, 3)], 1)
    p1, p3 = send_by_core(p0, 1, False), send_by_core(p0, 3, False)

    own = lax.all_to_all(parts, "gx", 0, 0, tiled=True)
    p1, p3, own = lax.optimization_barrier((p1, p3, own))
    p2p, p2m = send_by_core(p1[:1], 1, False), send_by_core(p3[1:], 3, False)
    pieces = p0, p1, p3, p2p, p2m
    far = swap_z_lo(own)

    def input_part(*given):
        count = sum(p.shape[0] for p in given)
        return call(
            functools.partial(input_body, len(given)),
            [((count, 2) + block, bf16)] * 2,
            [SMEM, VMEM] + [ANY] * len(given),
            (product * count // 8, 2 * (4 * rows * features + count * (4 * rows + features) * tokens)),
            out_specs=[ANY] * 2,
            scratch=[
                pltpu.VMEM((count, 4, tokens // 4, features), bf16),
                pltpu.VMEM((2, 2, 2) + block, bf16),
                pltpu.SemaphoreType.DMA((count,)),
                pltpu.SemaphoreType.DMA((2, 2)),
            ],
        )(at, w, *given)

    mine, theirs = input_part(p0, p1, p3)
    other = swap_core(theirs)
    mine2, theirs2 = input_part(p2p, p2m)
    size = 2 * 4 * rows * tokens
    (sums,) = call(
        core_sum_body,
        [((8, 2) + block, bf16)],
        [SMEM] + [VMEM] * 4,
        (4 * size, 12 * size),
        out_specs=[ANY],
        scratch=[pltpu.VMEM((8, 2) + block, bf16), pltpu.SemaphoreType.DMA((8,))],
    )(at, mine, mine2, other, swap_core(theirs2))
    same_core = [[2 * (2 * i + k) + c for i in range(8) for k in range(2)] for c in range(2)]
    back = lax.all_to_all(
        sums.reshape((16,) + block), ("gx", "gz"), 0, 0, tiled=True, axis_index_groups=same_core
    )
    own, far, _ = lax.optimization_barrier((own, far, sums))
    hidden = [own, far, swap_core(own), swap_core(far)]
    (weight_grad,) = call(
        weight_body,
        [((4 * rows, features), bf16)],
        [SMEM] + [VMEM] * 4 + [ANY] * 5,
        (product, 2 * (8 * rows * features + 2048 * features)),
        scratch=grad_scratch,
    )(at, *hidden, *pieces)
    back, weight_grad = lax.optimization_barrier((back, weight_grad))
    (pre_grad,) = call(
        finish_body,
        [((tokens, columns), bf16)],
        [SMEM] + [VMEM] * 2,
        (2 * tokens * 256 * columns, 8 * tokens * columns),
    )(at, slope, back.reshape((8, 2) + block))
    return pre_grad, weight_grad.reshape(weight.shape)


def solution(mesh):
    placed = (P("gx", ("gy", "gz")), P(("gx", "gy"), "gz"), P("gy", "gx", "gz"))
    return jax.shard_map(
        per_device,
        mesh=mesh,
        in_specs=placed,
        out_specs=(P("gx", ("gy", "gz")), P("gy", "gx", "gz")),
        check_vma=False,
    )
```

```python
import functools

import jax
import jax.numpy as jnp
from jax import lax
from jax.experimental import pallas as pl
from jax.experimental.pallas import tpu as pltpu
from jax.sharding import PartitionSpec as P

tanh_scale = 0.7978845608028654
cubic_coef = 0.044715
bf16 = jnp.bfloat16
f32 = jnp.float32
MIB = 1024 * 1024
VMEM = pl.BlockSpec(memory_space=pltpu.VMEM)
SMEM = pl.BlockSpec(memory_space=pltpu.SMEM)
HBM = pl.BlockSpec(memory_space=pltpu.HBM)


def send(v, axis, count, to):
    return lax.ppermute(v, axis, [(i, to(i)) for i in range(count)])


def send_x(v, d):
    return send(v, "gx", 8, lambda i: ((i // 2 + d) % 4) * 2 + i % 2)


def send_y(v, d):
    return send(v, "gy", 4, lambda i: (i + d) % 4)


def swap_z_hi(v):
    return send(v, "gx", 8, lambda i: i ^ 1)


def swap_z_lo(v):
    return send(v, "gz", 4, lambda i: i ^ 2)


def swap_core(v):
    return send(v, "gz", 4, lambda i: i ^ 1)


def send_by_core(v, d, first):
    pairs = []
    for i in range(128):
        x, z_hi, y, z_lo, core = i // 32, i // 16 % 2, i // 4 % 4, i // 2 % 2, i % 2
        if (core == 0) == first:
            y = (y + d) % 4
        else:
            x = (x + d) % 4
        pairs.append((i, (((x * 2 + z_hi) * 4 + y) * 2 + z_lo) * 2 + core))
    return lax.ppermute(v, ("gx", "gy", "gz"), pairs)


def call(body, out_shape, in_specs, cost, out_specs=None, scratch=(), limit=56):
    if out_specs is None:
        out_specs = [VMEM] * len(out_shape)
    flops, moved = cost
    return pl.pallas_call(
        body,
        out_shape=[jax.ShapeDtypeStruct(*s) for s in out_shape],
        in_specs=in_specs,
        out_specs=out_specs,
        scratch_shapes=list(scratch),
        compiler_params=pltpu.CompilerParams(vmem_limit_bytes=limit * MIB),
        cost_estimate=pl.CostEstimate(flops=flops, bytes_accessed=moved, transcendentals=0),
    )


def one_hot():
    q = lax.broadcasted_iota(jnp.int32, (256, 256), 0)
    u = lax.broadcasted_iota(jnp.int32, (256, 256), 1)
    return jnp.where(u == (q % 32) * 8 + q // 32, 1.0, 0.0).astype(bf16)


def group(at, k, z):
    return ((at[0] - k) & 3) * 2 + (at[1] ^ z)


def token_rows(y, k):
    return pl.ds(pl.multiple_of(((y - k) & 3) * 64, 64), 64)


def pack_body(at, pre, *outs):
    slope, parts = outs
    pick = one_hot()
    for j in range(pre.shape[1] // 256):
        cols = slice(256 * j, 256 * j + 256)
        u = jnp.concatenate([pre[token_rows(at[2], k), cols] for k in range(4)], 0)
        u = u.astype(f32)
        t = jnp.tanh(tanh_scale * (u + cubic_coef * u * u * u))
        slope[:, cols] = 0.5 * (1.0 + t) + 0.5 * u * (1.0 - t * t) * tanh_scale * (
            1.0 + 3.0 * cubic_coef * u * u
        )
        hidden = (0.5 * u * (1.0 + t)).astype(bf16)
        turned = lax.dot_general(pick, hidden, (((1,), (1,)), ((), ())), preferred_element_type=f32)
        turned = turned.astype(bf16)
        for i in range(8):
            parts[i, 32 * j : 32 * j + 32, :] = turned[32 * i : 32 * i + 32, :]


def load_grads(at, pieces, held, sems):
    p0, p1, p3, p2p, p2m = pieces
    todo = [(p0, 0, 0), (p0, 0, 1), (p1, 1, 0), (p1, 1, 1), (p3, 3, 0), (p3, 3, 1), (p2p, 2, 0), (p2m, 2, 1)]

    def copies(core):
        made = []
        for n, (src, k, z) in enumerate(todo):
            src = src.at[z if src.shape[0] == 2 else 0]
            dst = held.at[k, z] if core == 0 else held.at[:, z, k]
            made.append(pltpu.make_async_copy(src, dst, sems.at[n]))
        return made

    for core in range(2):

        @pl.when(at[4] == core)
        def _():
            for c in copies(core):
                c.start()
            for c in copies(core):
                c.wait()


def input_body(count, at, w, *refs):
    pieces, (mine, theirs, held, sums, in_sems, out_sems) = refs[:count], refs[count:]
    blocks = [p.at[z] for p in pieces for z in range(p.shape[0])]
    for i, src in enumerate(blocks):
        pltpu.make_async_copy(src, held.at[i], in_sems.at[i]).start()
    rows = w.shape[0] // 4

    def leaving(i):
        slot = i % 2
        return [
            pltpu.make_async_copy(sums.at[slot, n], out.at[i], out_sems.at[slot, n])
            for n, out in enumerate((mine, theirs))
        ]

    @pl.loop(0, len(blocks))
    def _(i):
        pltpu.make_async_copy(blocks[0], held.at[i], in_sems.at[i]).wait()

        @pl.when(i >= 2)
        def _():
            for c in leaving(i - 2):
                c.wait()

        part = lax.dot_general(
            w[...], held[i].reshape(256, -1), (((1,), (1,)), ((), ())), preferred_element_type=f32
        ).astype(bf16)
        for n in range(4):
            sums[i % 2, at[4] ^ (n % 2), n // 2] = part[n * rows : n * rows + rows]
        for c in leaving(i):
            c.start()

    for i in range(len(blocks) - 2, len(blocks)):
        for c in leaving(i):
            c.wait()


def core_sum_body(at, mine, mine2, other, other2, out, held, sems):
    def leaving(k, z):
        n = 2 * k + z
        return pltpu.make_async_copy(held.at[n], out.at[group(at, k, z)], sems.at[n])

    def block(early, late, k, z, lo):
        if k == 2:
            return late[z, lo]
        return early[2 * (k - k // 3) + z, lo]

    for core in range(2):

        @pl.when(at[4] == core)
        def _():
            by_x, by_y = (mine, mine2), (other, other2)
            if core:
                by_x, by_y = by_y, by_x
            for z in range(2):
                for lo in range(2):
                    y = [block(*by_y, k, z, lo) for k in range(4)]
                    for k in range(4):
                        turned = jnp.concatenate([v[:, 64 * k : 64 * k + 64] for v in y], 1)
                        total = block(*by_x, k, z, lo).astype(f32) + turned.astype(f32)
                        held[2 * k + z, lo] = total.astype(bf16)
                for k in range(4):
                    leaving(k, z).start()

    for z in range(2):
        for k in range(4):
            leaving(k, z).wait()


def finish_body(at, slope, parts, out):
    pick = one_hot()
    for j in range(out.shape[1] // 256):
        cols, units = slice(256 * j, 256 * j + 256), slice(32 * j, 32 * j + 32)
        v = [(parts[n, 0, units, :].astype(f32) + parts[n, 1, units, :].astype(f32)) for n in range(8)]
        v = jnp.concatenate(v, 0).astype(bf16)
        total = lax.dot_general(v, pick, (((0,), (0,)), ((), ())), preferred_element_type=f32)
        result = (total * slope[:, cols]).astype(bf16)
        for k in range(4):
            out[token_rows(at[2], k), cols] = result[64 * k : 64 * k + 64, :]


def weight_body(at, *refs):
    hidden, pieces, (out, held, sems) = refs[:4], refs[4:9], refs[9:]
    load_grads(at, pieces, held, sems)
    rows = out.shape[0] // 4
    lhs = jnp.concatenate(
        [jnp.concatenate([h[group(at, k, z)] for k in range(4) for z in range(2)], 1) for h in hidden], 0
    )

    @pl.loop(0, out.shape[1] // 256)
    def _(j):
        cols = pl.ds(pl.multiple_of(j * 256, 256), 256)
        grads = held[:, :, :, :, cols].reshape(2048, 256)
        total = lax.dot_general(lhs, grads, (((1,), (0,)), ((), ())), preferred_element_type=f32)
        total = total.astype(bf16)
        for n, (lo, core) in enumerate(((0, 0), (1, 0), (0, 1), (1, 1))):
            block = ((at[3] + lo) & 1) * 2 + ((at[4] + core) & 1)
            out[pl.ds(pl.multiple_of(block * rows, 64), rows), cols] = total[n * rows : n * rows + rows]


def per_device(pre_act, grad_out, weight):
    tokens, columns = pre_act.shape
    rows, features = columns // 8, grad_out.shape[1]
    gx, y, gz = lax.axis_index("gx"), lax.axis_index("gy"), lax.axis_index("gz")
    at = jnp.stack([gx // 2, gx % 2, y, gz // 2, gz % 2]).astype(jnp.int32)
    w = weight.reshape(4 * rows, features)
    block = (rows, tokens)
    grad_scratch = [pltpu.VMEM((4, 2, 4, tokens // 4, features), bf16), pltpu.SemaphoreType.DMA((8,))]
    product = 2 * 4 * rows * 8 * tokens * features

    slope, parts = call(
        pack_body,
        [((tokens, columns), f32), ((8,) + block, bf16)],
        [SMEM, VMEM],
        (2 * tokens * 256 * columns, 8 * tokens * columns),
    )(at, pre_act)

    other, parts = lax.optimization_barrier((swap_z_hi(grad_out), parts))
    both = jnp.stack([grad_out, other])
    first = [send_by_core(both, k, True) for k in (1, 2, 3)]
    own = lax.all_to_all(parts, "gx", 0, 0, tiled=True)
    first, own = lax.optimization_barrier((first, own))
    p0 = jnp.stack([both] + first, 1)
    p1, p3 = send_by_core(p0, 1, False), send_by_core(p0, 3, False)

    p2p, p2m = send_by_core(p1[:1], 1, False), send_by_core(p3[1:], 3, False)
    pieces = p0, p1, p3, p2p, p2m
    far = swap_z_lo(own)

    def input_part(*given):
        count = sum(p.shape[0] for p in given)
        return call(
            functools.partial(input_body, len(given)),
            [((count, 2) + block, bf16)] * 2,
            [SMEM, VMEM] + [HBM] * len(given),
            (product * count // 8, 2 * (4 * rows * features + count * (4 * rows + features) * tokens)),
            out_specs=[HBM] * 2,
            scratch=[
                pltpu.VMEM((count, 4, tokens // 4, features), bf16),
                pltpu.VMEM((2, 2, 2) + block, bf16),
                pltpu.SemaphoreType.DMA((count,)),
                pltpu.SemaphoreType.DMA((2, 2)),
            ],
        )(at, w, *given)

    early = lax.optimization_barrier((p0, p1, p3, far))
    mine, theirs = input_part(*early[:3])
    other = swap_core(theirs)
    hidden = [own, far, swap_core(own), swap_core(far)]
    p2p, p2m, hidden = lax.optimization_barrier((p2p, p2m, hidden))
    mine2, theirs2 = input_part(p2p, p2m)
    size = 2 * 4 * rows * tokens
    (sums,) = call(
        core_sum_body,
        [((8, 2) + block, bf16)],
        [SMEM] + [VMEM] * 4,
        (4 * size, 12 * size),
        out_specs=[HBM],
        scratch=[pltpu.VMEM((8, 2) + block, bf16), pltpu.SemaphoreType.DMA((8,))],
    )(at, mine, mine2, other, swap_core(theirs2))
    same_core = [[2 * (2 * i + k) + c for i in range(8) for k in range(2)] for c in range(2)]
    back = lax.all_to_all(
        sums.reshape((16,) + block), ("gx", "gz"), 0, 0, tiled=True, axis_index_groups=same_core
    )
    hidden, _ = lax.optimization_barrier((hidden, sums))
    (weight_grad,) = call(
        weight_body,
        [((4 * rows, features), bf16)],
        [SMEM] + [VMEM] * 4 + [HBM] * 5,
        (product, 2 * (8 * rows * features + 2048 * features)),
        scratch=grad_scratch,
    )(at, *hidden, *pieces)
    back, weight_grad = lax.optimization_barrier((back, weight_grad))
    (pre_grad,) = call(
        finish_body,
        [((tokens, columns), bf16)],
        [SMEM] + [VMEM] * 2,
        (2 * tokens * 256 * columns, 8 * tokens * columns),
    )(at, slope, back.reshape((8, 2) + block))
    return pre_grad, weight_grad.reshape(weight.shape)


def solution(mesh):
    placed = (P("gx", ("gy", "gz")), P(("gx", "gy"), "gz"), P("gy", "gx", "gz"))
    return jax.shard_map(
        per_device,
        mesh=mesh,
        in_specs=placed,
        out_specs=(P("gx", ("gy", "gz")), P("gy", "gx", "gz")),
        check_vma=False,
    )
```

```python
import functools

import jax
import jax.numpy as jnp
from jax import lax
from jax.experimental import pallas as pl
from jax.experimental.pallas import tpu as pltpu
from jax.sharding import PartitionSpec as P

tanh_scale = 0.7978845608028654
cubic_coef = 0.044715
bf16 = jnp.bfloat16
f32 = jnp.float32
MIB = 1024 * 1024
VMEM = pl.BlockSpec(memory_space=pltpu.VMEM)
SMEM = pl.BlockSpec(memory_space=pltpu.SMEM)
HBM = pl.BlockSpec(memory_space=pltpu.HBM)


def send(v, axis, count, to):
    return lax.ppermute(v, axis, [(i, to(i)) for i in range(count)])


def send_x(v, d):
    return send(v, "gx", 8, lambda i: ((i // 2 + d) % 4) * 2 + i % 2)


def send_y(v, d):
    return send(v, "gy", 4, lambda i: (i + d) % 4)


def swap_z_hi(v):
    return send(v, "gx", 8, lambda i: i ^ 1)


def swap_z_lo(v):
    return send(v, "gz", 4, lambda i: i ^ 2)


def swap_core(v):
    return send(v, "gz", 4, lambda i: i ^ 1)


def send_by_core(v, d, first):
    pairs = []
    for i in range(128):
        x, z_hi, y, z_lo, core = i // 32, i // 16 % 2, i // 4 % 4, i // 2 % 2, i % 2
        if (core == 0) == first:
            y = (y + d) % 4
        else:
            x = (x + d) % 4
        pairs.append((i, (((x * 2 + z_hi) * 4 + y) * 2 + z_lo) * 2 + core))
    return lax.ppermute(v, ("gx", "gy", "gz"), pairs)


def call(body, out_shape, in_specs, cost, out_specs=None, scratch=(), aliases={}, limit=56):
    if out_specs is None:
        out_specs = [VMEM] * len(out_shape)
    flops, moved = cost
    return pl.pallas_call(
        body,
        out_shape=[jax.ShapeDtypeStruct(*s) for s in out_shape],
        in_specs=in_specs,
        out_specs=out_specs,
        scratch_shapes=list(scratch),
        input_output_aliases=aliases,
        compiler_params=pltpu.CompilerParams(vmem_limit_bytes=limit * MIB),
        cost_estimate=pl.CostEstimate(flops=flops, bytes_accessed=moved, transcendentals=0),
    )


def one_hot():
    q = lax.broadcasted_iota(jnp.int32, (256, 256), 0)
    u = lax.broadcasted_iota(jnp.int32, (256, 256), 1)
    return jnp.where(u == (q % 32) * 8 + q // 32, 1.0, 0.0).astype(bf16)


def group(at, k, z):
    return ((at[0] - k) & 3) * 2 + (at[1] ^ z)


def token_rows(y, k):
    return pl.ds(pl.multiple_of(((y - k) & 3) * 64, 64), 64)


def pack_body(at, pre, *outs):
    slope, parts = outs
    pick = one_hot()
    for j in range(pre.shape[1] // 256):
        cols = slice(256 * j, 256 * j + 256)
        u = jnp.concatenate([pre[token_rows(at[2], k), cols] for k in range(4)], 0)
        u = u.astype(f32)
        t = jnp.tanh(tanh_scale * (u + cubic_coef * u * u * u))
        slope[:, cols] = 0.5 * (1.0 + t) + 0.5 * u * (1.0 - t * t) * tanh_scale * (
            1.0 + 3.0 * cubic_coef * u * u
        )
        hidden = (0.5 * u * (1.0 + t)).astype(bf16)
        turned = lax.dot_general(pick, hidden, (((1,), (1,)), ((), ())), preferred_element_type=f32)
        turned = turned.astype(bf16)
        for i in range(8):
            parts[i, 32 * j : 32 * j + 32, :] = turned[32 * i : 32 * i + 32, :]


def load_grads(at, pieces, held, sems):
    low, high, full = pl.ds(0, 2), pl.ds(2, 2), pl.ds(0, 4)
    p0, p1, p3, r0, up, down, r2p, r2m = pieces
    todo = [(p0, 0, 0, full), (p1, 1, 0, full), (p3, 3, 0, full), (up.at[low], 2, 0, low), (down.at[low], 2, 0, high)]
    todo += [(r0, 0, 1, full), (up.at[pl.ds(2, 4)], 1, 1, full), (down.at[pl.ds(2, 4)], 3, 1, full)]
    todo += [(r2p, 2, 1, low), (r2m, 2, 1, high)]

    def copies(core):
        made = []
        for n, (src, k, z, part) in enumerate(todo):
            dst = held.at[k, z, part] if core == 0 else held.at[part, z, k]
            made.append(pltpu.make_async_copy(src, dst, sems.at[n]))
        return made

    for core in range(2):

        @pl.when(at[4] == core)
        def _():
            for c in copies(core):
                c.start()
            for c in copies(core):
                c.wait()


def input_body(halves, at, w_hbm, *refs):
    count = len(halves) // 2
    pieces, (mine, theirs, w, held, sums, w_sem, in_sems, out_sems) = refs[:-8], refs[-8:]
    load = pltpu.make_async_copy(w_hbm, w, w_sem)
    load.start()
    sources = [pieces[n].at[pl.ds(start, 2)] for n, start in halves]

    def coming(i, half, src):
        return pltpu.make_async_copy(src, held.at[i, pl.ds(2 * half, 2)], in_sems.at[i, half])

    def leaving(i):
        slot = i % 2
        return [
            pltpu.make_async_copy(sums.at[slot, at[4] ^ n], out.at[i], out_sems.at[slot, n])
            for n, out in enumerate((mine, theirs))
        ]

    for n, src in enumerate(sources):
        coming(n // 2, n % 2, src).start()
    load.wait()
    rows = w.shape[0] // 4

    @pl.loop(0, count)
    def _(i):
        for half in range(2):
            coming(i, half, sources[half]).wait()

        @pl.when(i >= 2)
        def _():
            for c in leaving(i - 2):
                c.wait()

        part = lax.dot_general(
            w[...], held[i].reshape(256, -1), (((1,), (1,)), ((), ())), preferred_element_type=f32
        ).astype(bf16)
        for n in range(4):
            sums[i % 2, n % 2, n // 2] = part[n * rows : n * rows + rows]
        for c in leaving(i):
            c.start()

    for i in range(max(count - 2, 0), count):
        for c in leaving(i):
            c.wait()


def core_sum_body(z, places, at, *refs):
    mine, other, (out, held, sems) = refs[: len(refs) // 2 - 1 - z], refs[len(refs) // 2 - 1 - z : -3 - z], refs[-3:]

    def leaving(k):
        return pltpu.make_async_copy(held.at[k], out.at[group(at, k, z)], sems.at[k])

    for core in range(2):

        @pl.when(at[4] == core)
        def _():
            by_x, by_y = (other, mine) if core else (mine, other)
            for lo in range(2):
                for k, (n, i) in enumerate(places):
                    turned = jnp.concatenate([by_y[m][j, lo, :, 64 * k : 64 * k + 64] for m, j in places], 1)
                    held[k, lo] = (by_x[n][i, lo].astype(f32) + turned.astype(f32)).astype(bf16)
                    if lo:
                        leaving(k).start()

    for k in range(4):
        leaving(k).wait()


def finish_body(at, slope, parts, out):
    pick = one_hot()
    for j in range(out.shape[1] // 256):
        cols, units = slice(256 * j, 256 * j + 256), slice(32 * j, 32 * j + 32)
        v = [(parts[n, 0, units, :].astype(f32) + parts[n, 1, units, :].astype(f32)) for n in range(8)]
        v = jnp.concatenate(v, 0).astype(bf16)
        total = lax.dot_general(v, pick, (((0,), (0,)), ((), ())), preferred_element_type=f32)
        result = (total * slope[:, cols]).astype(bf16)
        for k in range(4):
            out[token_rows(at[2], k), cols] = result[64 * k : 64 * k + 64, :]


def weight_body(at, *refs):
    hidden, pieces, (out, held, sems) = refs[:4], refs[4:12], refs[12:]
    load_grads(at, pieces, held, sems)
    rows = out.shape[0] // 4
    lhs = jnp.concatenate(
        [jnp.concatenate([h[group(at, k, z)] for k in range(4) for z in range(2)], 1) for h in hidden], 0
    )

    @pl.loop(0, out.shape[1] // 256)
    def _(j):
        cols = pl.ds(pl.multiple_of(j * 256, 256), 256)
        grads = held[:, :, :, :, cols].reshape(2048, 256)
        total = lax.dot_general(lhs, grads, (((1,), (0,)), ((), ())), preferred_element_type=f32)
        total = total.astype(bf16)
        for n, (lo, core) in enumerate(((0, 0), (1, 0), (0, 1), (1, 1))):
            block = ((at[3] + lo) & 1) * 2 + ((at[4] + core) & 1)
            out[pl.ds(pl.multiple_of(block * rows, 64), rows), cols] = total[n * rows : n * rows + rows]


def per_device(pre_act, grad_out, weight):
    tokens, columns = pre_act.shape
    rows, features = columns // 8, grad_out.shape[1]
    gx, y, gz = lax.axis_index("gx"), lax.axis_index("gy"), lax.axis_index("gz")
    at = jnp.stack([gx // 2, gx % 2, y, gz // 2, gz % 2]).astype(jnp.int32)
    w = weight.reshape(4 * rows, features)
    block = (rows, tokens)
    grad_scratch = [pltpu.VMEM((4, 2, 4, tokens // 4, features), bf16), pltpu.SemaphoreType.DMA((10,))]
    product = 2 * 4 * rows * 8 * tokens * features

    slope, parts = call(
        pack_body,
        [((tokens, columns), f32), ((8,) + block, bf16)],
        [SMEM, VMEM],
        (2 * tokens * 256 * columns, 8 * tokens * columns),
    )(at, pre_act)

    other = swap_z_hi(grad_out)
    first = [send_by_core(grad_out, k, True) for k in (1, 2, 3)]
    first, other = lax.optimization_barrier((first, other))
    p0 = jnp.stack([grad_out] + first)
    p1, p3 = send_by_core(p0, 1, False), send_by_core(p0, 3, False)
    r0 = jnp.stack([other] + [send_by_core(other, k, True) for k in (1, 2, 3)])
    p1, p3, r0, parts = lax.optimization_barrier((p1, p3, r0, parts))
    up = send_by_core(jnp.concatenate([p1[:2], r0]), 1, False)
    down = send_by_core(jnp.concatenate([p3[2:], r0]), 3, False)
    own = lax.all_to_all(parts, "gx", 0, 0, tiled=True)
    def input_part(halves, *given):
        count = len(halves) // 2
        return call(
            functools.partial(input_body, halves),
            [((count, 2) + block, bf16)] * 2,
            [SMEM, HBM] + [HBM] * len(given),
            (product * count // 8, 2 * (4 * rows * features + count * (4 * rows + features) * tokens)),
            out_specs=[HBM] * 2,
            scratch=[
                pltpu.VMEM((4 * rows, features), bf16),
                pltpu.VMEM((count, 4, tokens // 4, features), bf16),
                pltpu.VMEM((2, 2, 2) + block, bf16),
                pltpu.SemaphoreType.DMA,
                pltpu.SemaphoreType.DMA((count, 2)),
                pltpu.SemaphoreType.DMA((2, 2)),
            ],
        )(at, w, *given)

    def core_sum(z, places, mine, other, *into):
        return call(
            functools.partial(core_sum_body, z, places),
            [((8, 2) + block, bf16)],
            [SMEM] + [VMEM] * (2 * len(mine)) + [HBM] * len(into),
            (8 * rows * tokens, 24 * rows * tokens),
            out_specs=[HBM],
            scratch=[pltpu.VMEM((4, 2) + block, bf16), pltpu.SemaphoreType.DMA((4,))],
            aliases={1 + 2 * len(mine): 0} if into else {},
        )(at, *mine, *other, *into)[0]

    mine0, theirs0 = input_part([(n, at) for n in range(3) for at in (0, 2)], p0, p1, p3)
    up, down, other0, own = lax.optimization_barrier((up, down, swap_core(theirs0), own))
    r2p, r2m = send_by_core(up[2:4], 1, False), send_by_core(down[4:], 3, False)
    pieces = p0, p1, p3, r0, up, down, r2p, r2m
    mine1, theirs1 = input_part(
        [(1, 0), (2, 0), (0, 0), (0, 2), (1, 2), (1, 4), (2, 2), (2, 4)], r0, up, down
    )
    far = swap_z_lo(own)
    mine2, theirs2 = input_part([(0, 0), (1, 0)], r2p, r2m)
    theirs1, _ = lax.optimization_barrier((theirs1, theirs2))
    other1 = swap_core(theirs1)
    sums = core_sum(0, ((0, 0), (0, 1), (1, 0), (0, 2)), [mine0, mine1], [other0, other1])
    sums = core_sum(
        1,
        ((0, 1), (0, 2), (1, 0), (0, 3)),
        [mine1, mine2],
        [other1, swap_core(theirs2)],
        sums,
    )
    own, far, _ = lax.optimization_barrier((own, far, sums))
    hidden = [own, far, swap_core(own), swap_core(far)]
    same_core = [[2 * (2 * i + k) + c for i in range(8) for k in range(2)] for c in range(2)]
    back = lax.all_to_all(
        sums.reshape((16,) + block), ("gx", "gz"), 0, 0, tiled=True, axis_index_groups=same_core
    )
    (weight_grad,) = call(
        weight_body,
        [((4 * rows, features), bf16)],
        [SMEM] + [VMEM] * 4 + [HBM] * 8,
        (product, 2 * (8 * rows * features + 2048 * features)),
        scratch=grad_scratch,
    )(at, *hidden, *pieces)
    back, weight_grad = lax.optimization_barrier((back, weight_grad))
    (pre_grad,) = call(
        finish_body,
        [((tokens, columns), bf16)],
        [SMEM] + [VMEM] * 2,
        (2 * tokens * 256 * columns, 8 * tokens * columns),
    )(at, slope, back.reshape((8, 2) + block))
    return pre_grad, weight_grad.reshape(weight.shape)


def solution(mesh):
    placed = (P("gx", ("gy", "gz")), P(("gx", "gy"), "gz"), P("gy", "gx", "gz"))
    return jax.shard_map(
        per_device,
        mesh=mesh,
        in_specs=placed,
        out_specs=(P("gx", ("gy", "gz")), P("gy", "gx", "gz")),
        check_vma=False,
    )
```

```python
import functools

import jax
import jax.numpy as jnp
from jax import lax
from jax.experimental import pallas as pl
from jax.experimental.pallas import tpu as pltpu
from jax.sharding import PartitionSpec as P

tanh_scale = 0.7978845608028654
cubic_coef = 0.044715
bf16 = jnp.bfloat16
f32 = jnp.float32
MIB = 1024 * 1024
VMEM = pl.BlockSpec(memory_space=pltpu.VMEM)
SMEM = pl.BlockSpec(memory_space=pltpu.SMEM)
HBM = pl.BlockSpec(memory_space=pltpu.HBM)


def send(v, axis, count, to):
    return lax.ppermute(v, axis, [(i, to(i)) for i in range(count)])


def send_x(v, d):
    return send(v, "gx", 8, lambda i: ((i // 2 + d) % 4) * 2 + i % 2)


def send_y(v, d):
    return send(v, "gy", 4, lambda i: (i + d) % 4)


def swap_z_hi(v):
    return send(v, "gx", 8, lambda i: i ^ 1)


def swap_z_lo(v):
    return send(v, "gz", 4, lambda i: i ^ 2)


def swap_core(v):
    return send(v, "gz", 4, lambda i: i ^ 1)


def send_by_core(v, d, first):
    pairs = []
    for i in range(128):
        x, z_hi, y, z_lo, core = i // 32, i // 16 % 2, i // 4 % 4, i // 2 % 2, i % 2
        if (core == 0) == first:
            y = (y + d) % 4
        else:
            x = (x + d) % 4
        pairs.append((i, (((x * 2 + z_hi) * 4 + y) * 2 + z_lo) * 2 + core))
    return lax.ppermute(v, ("gx", "gy", "gz"), pairs)


def call(body, out_shape, in_specs, cost, out_specs=None, scratch=(), grid=(), limit=56):
    if out_specs is None:
        out_specs = [VMEM] * len(out_shape)
    flops, moved = cost
    return pl.pallas_call(
        body,
        grid=grid,
        out_shape=[jax.ShapeDtypeStruct(*s) for s in out_shape],
        in_specs=in_specs,
        out_specs=out_specs,
        scratch_shapes=list(scratch),
        compiler_params=pltpu.CompilerParams(vmem_limit_bytes=limit * MIB),
        cost_estimate=pl.CostEstimate(flops=flops, bytes_accessed=moved, transcendentals=0),
    )


def one_hot(at=None):
    q = lax.broadcasted_iota(jnp.int32, (256, 256), 0)
    u = lax.broadcasted_iota(jnp.int32, (256, 256), 1)
    s = q // 32
    if at is not None:
        s = ((at[0] - s // 2) & 3) * 2 + ((at[1] + s) & 1)
    return jnp.where(u == (q % 32) * 8 + s, 1.0, 0.0).astype(bf16)


def group(at, k, z):
    return ((at[0] - k) & 3) * 2 + (at[1] ^ z)


def token_rows(y, k):
    return pl.ds(pl.multiple_of(((y - k) & 3) * 64, 64), 64)


def pack_body(at, pre, *outs):
    slope, parts = outs[0], outs[1:]
    pick = one_hot(at)
    for j in range(pre.shape[1] // 256):
        cols = slice(256 * j, 256 * j + 256)
        u = jnp.concatenate([pre[token_rows(at[2], k), cols] for k in range(4)], 0)
        u = u.astype(f32)
        t = jnp.tanh(tanh_scale * (u + cubic_coef * u * u * u))
        slope[:, cols] = 0.5 * (1.0 + t) + 0.5 * u * (1.0 - t * t) * tanh_scale * (
            1.0 + 3.0 * cubic_coef * u * u
        )
        hidden = (0.5 * u * (1.0 + t)).astype(bf16)
        turned = lax.dot_general(pick, hidden, (((1,), (1,)), ((), ())), preferred_element_type=f32)
        turned = turned.astype(bf16)
        for i in range(8):
            parts[i // 2][i % 2, 32 * j : 32 * j + 32, :] = turned[32 * i : 32 * i + 32, :]


def load_grads(at, pieces, held, sems):
    p0, p1, p3, p2p, p2m = pieces
    todo = [(p0, 0, 0), (p0, 0, 1), (p1, 1, 0), (p1, 1, 1), (p3, 3, 0), (p3, 3, 1), (p2p, 2, 0), (p2m, 2, 1)]

    def copies(core):
        made = []
        for n, (src, k, z) in enumerate(todo):
            src = src.at[z if src.shape[0] == 2 else 0]
            dst = held.at[k, z] if core == 0 else held.at[:, z, k]
            made.append(pltpu.make_async_copy(src, dst, sems.at[n]))
        return made

    for core in range(2):

        @pl.when(at[4] == core)
        def _():
            for c in copies(core):
                c.start()
            for c in copies(core):
                c.wait()


def input_body(count, at, w_hbm, *refs):
    pieces, (mine, theirs, w, held, sums, w_sem, in_sems, out_sems) = refs[:count], refs[count:]
    load = pltpu.make_async_copy(w_hbm, w, w_sem)
    load.start()
    blocks = [p.at[z] for p in pieces for z in range(p.shape[0])]
    for i, src in enumerate(blocks):
        pltpu.make_async_copy(src, held.at[i], in_sems.at[i]).start()
    load.wait()
    rows = w.shape[0] // 4

    def leaving(i):
        slot = i % 2
        return [
            pltpu.make_async_copy(sums.at[slot, at[4] ^ n], out.at[i], out_sems.at[slot, n])
            for n, out in enumerate((mine, theirs))
        ]

    @pl.loop(0, len(blocks))
    def _(i):
        pltpu.make_async_copy(blocks[0], held.at[i], in_sems.at[i]).wait()

        @pl.when(i >= 2)
        def _():
            for c in leaving(i - 2):
                c.wait()

        part = lax.dot_general(
            w[...], held[i].reshape(256, -1), (((1,), (1,)), ((), ())), preferred_element_type=f32
        ).astype(bf16)
        for n in range(4):
            sums[i % 2, n % 2, n // 2] = part[n * rows : n * rows + rows]
        for c in leaving(i):
            c.start()

    for i in range(len(blocks) - 2, len(blocks)):
        for c in leaving(i):
            c.wait()


def core_sum_body(at, mine, mine2, other, other2, out, held, sems):
    def leaving(k, z):
        n = 2 * k + z
        return pltpu.make_async_copy(held.at[n], out.at[group(at, k, z)], sems.at[n])

    def block(early, late, k, z, lo, lanes=slice(None)):
        if k == 2:
            return late[z, lo, :, lanes]
        return early[2 * (k - k // 3) + z, lo, :, lanes]

    for core in range(2):

        @pl.when(at[4] == core)
        def _():
            by_x, by_y = (mine, mine2), (other, other2)
            if core:
                by_x, by_y = by_y, by_x
            for z in range(2):
                for lo in range(2):
                    for k in range(4):
                        lanes = pl.ds(64 * k, 64)
                        turned = jnp.concatenate([block(*by_y, n, z, lo, lanes) for n in range(4)], 1)
                        total = block(*by_x, k, z, lo).astype(f32) + turned.astype(f32)
                        held[2 * k + z, lo] = total.astype(bf16)
                for k in range(4):
                    leaving(k, z).start()

    for z in range(2):
        for k in range(4):
            leaving(k, z).wait()


def finish_body(at, slope, parts, out):
    v = [parts[n, 0].astype(f32) + parts[n, 1].astype(f32) for n in range(8)]
    v = jnp.concatenate(v, 0).astype(bf16)
    total = lax.dot_general(v, one_hot(), (((0,), (0,)), ((), ())), preferred_element_type=f32)
    result = (total * slope[...]).astype(bf16)
    for k in range(4):
        out[token_rows(at[2], k), :] = result[64 * k : 64 * k + 64, :]


def weight_body(at, *refs):
    hidden, pieces, (out, held, sems) = refs[:4], refs[4:9], refs[9:]
    load_grads(at, pieces, held, sems)
    rows = out.shape[0] // 4
    lhs = jnp.concatenate(
        [jnp.concatenate([h[z, k] for k in range(4) for z in range(2)], 1) for h in hidden], 0
    )

    @pl.loop(0, out.shape[1] // 256)
    def _(j):
        cols = pl.ds(pl.multiple_of(j * 256, 256), 256)
        grads = held[:, :, :, :, cols].reshape(2048, 256)
        total = lax.dot_general(lhs, grads, (((1,), (0,)), ((), ())), preferred_element_type=f32)
        total = total.astype(bf16)
        for n, (lo, core) in enumerate(((0, 0), (1, 0), (0, 1), (1, 1))):
            block = ((at[3] + lo) & 1) * 2 + ((at[4] + core) & 1)
            out[pl.ds(pl.multiple_of(block * rows, 64), rows), cols] = total[n * rows : n * rows + rows]


def per_device(pre_act, grad_out, weight):
    tokens, columns = pre_act.shape
    rows, features = columns // 8, grad_out.shape[1]
    gx, y, gz = lax.axis_index("gx"), lax.axis_index("gy"), lax.axis_index("gz")
    at = jnp.stack([gx // 2, gx % 2, y, gz // 2, gz % 2]).astype(jnp.int32)
    w = weight.reshape(4 * rows, features)
    block = (rows, tokens)
    grad_scratch = [pltpu.VMEM((4, 2, 4, tokens // 4, features), bf16), pltpu.SemaphoreType.DMA((8,))]
    product = 2 * 4 * rows * 8 * tokens * features

    slope, *parts = call(
        pack_body,
        [((tokens, columns), f32)] + [((2,) + block, bf16)] * 4,
        [SMEM, VMEM],
        (2 * tokens * 256 * columns, 8 * tokens * columns),
    )(at, pre_act)

    other = swap_z_hi(grad_out)
    first = [[v] + [send_by_core(v, k, True) for k in (1, 2, 3)] for v in (grad_out, other)]

    by_x = [parts[0]] + [send_x(parts[4 - k], k) for k in (1, 2, 3)]
    first, by_x = lax.optimization_barrier((first, by_x))
    p0 = jnp.stack([jnp.stack(v) for v in first])
    p1, p3 = send_by_core(p0, 1, False), send_by_core(p0, 3, False)

    p2p, p2m = send_by_core(p1[:1], 1, False), send_by_core(p3[1:], 3, False)
    pieces = p0, p1, p3, p2p, p2m
    own = jnp.stack([p[0] for p in by_x])
    own = jnp.stack([own, swap_z_hi(jnp.stack([p[1] for p in by_x]))])
    far = swap_z_lo(own)

    def input_part(*given):
        count = sum(p.shape[0] for p in given)
        return call(
            functools.partial(input_body, len(given)),
            [((count, 2) + block, bf16)] * 2,
            [SMEM, HBM] + [HBM] * len(given),
            (product * count // 8, 2 * (4 * rows * features + count * (4 * rows + features) * tokens)),
            out_specs=[HBM] * 2,
            scratch=[
                pltpu.VMEM((4 * rows, features), bf16),
                pltpu.VMEM((count, 4, tokens // 4, features), bf16),
                pltpu.VMEM((2, 2, 2) + block, bf16),
                pltpu.SemaphoreType.DMA,
                pltpu.SemaphoreType.DMA((count,)),
                pltpu.SemaphoreType.DMA((2, 2)),
            ],
        )(at, w, *given)

    early = lax.optimization_barrier((p0, p1, p3, own))
    mine, theirs = input_part(*early[:3])
    other = swap_core(theirs)
    mine2, theirs2 = input_part(p2p, p2m)
    size = 2 * 4 * rows * tokens
    (sums,) = call(
        core_sum_body,
        [((8, 2) + block, bf16)],
        [SMEM] + [VMEM] * 4,
        (4 * size, 12 * size),
        out_specs=[HBM],
        scratch=[pltpu.VMEM((8, 2) + block, bf16), pltpu.SemaphoreType.DMA((8,))],
    )(at, mine, mine2, other, swap_core(theirs2))
    same_core = [[2 * (2 * i + k) + c for i in range(8) for k in range(2)] for c in range(2)]
    back = lax.all_to_all(
        sums.reshape((16,) + block), ("gx", "gz"), 0, 0, tiled=True, axis_index_groups=same_core
    )
    own, far, _ = lax.optimization_barrier((own, far, sums))
    hidden = [own, far, swap_core(own), swap_core(far)]
    (weight_grad,) = call(
        weight_body,
        [((4 * rows, features), bf16)],
        [SMEM] + [VMEM] * 4 + [HBM] * 5,
        (product, 2 * (8 * rows * features + 2048 * features)),
        scratch=grad_scratch,
    )(at, *hidden, *pieces)
    back, weight_grad = lax.optimization_barrier((back, weight_grad))
    (pre_grad,) = call(
        finish_body,
        [((tokens, columns), bf16)],
        [
            SMEM,
            pl.BlockSpec((tokens, 256), lambda j: (0, j)),
            pl.BlockSpec((8, 2, 32, tokens), lambda j: (0, 0, j, 0)),
        ],
        (2 * tokens * 256 * columns, 8 * tokens * columns),
        out_specs=[pl.BlockSpec((tokens, 256), lambda j: (0, j))],
        grid=(columns // 256,),
    )(at, slope, back.reshape((8, 2) + block))
    return pre_grad, weight_grad.reshape(weight.shape)


def solution(mesh):
    placed = (P("gx", ("gy", "gz")), P(("gx", "gy"), "gz"), P("gy", "gx", "gz"))
    return jax.shard_map(
        per_device,
        mesh=mesh,
        in_specs=placed,
        out_specs=(P("gx", ("gy", "gz")), P("gy", "gx", "gz")),
        check_vma=False,
    )
```

```python
import functools

import jax
import jax.numpy as jnp
from jax import lax
from jax.experimental import pallas as pl
from jax.experimental.pallas import tpu as pltpu
from jax.sharding import PartitionSpec as P

tanh_scale = 0.7978845608028654
cubic_coef = 0.044715
bf16 = jnp.bfloat16
f32 = jnp.float32
MIB = 1024 * 1024
VMEM = pl.BlockSpec(memory_space=pltpu.VMEM)
SMEM = pl.BlockSpec(memory_space=pltpu.SMEM)
HBM = pl.BlockSpec(memory_space=pltpu.HBM)


def send(v, axis, count, to):
    return lax.ppermute(v, axis, [(i, to(i)) for i in range(count)])


def send_x(v, d):
    return send(v, "gx", 8, lambda i: ((i // 2 + d) % 4) * 2 + i % 2)


def send_y(v, d):
    return send(v, "gy", 4, lambda i: (i + d) % 4)


def swap_z_hi(v):
    return send(v, "gx", 8, lambda i: i ^ 1)


def swap_z_lo(v):
    return send(v, "gz", 4, lambda i: i ^ 2)


def swap_core(v):
    return send(v, "gz", 4, lambda i: i ^ 1)


def send_by_core(v, d, first):
    pairs = []
    for i in range(128):
        x, z_hi, y, z_lo, core = i // 32, i // 16 % 2, i // 4 % 4, i // 2 % 2, i % 2
        if (core == 0) == first:
            y = (y + d) % 4
        else:
            x = (x + d) % 4
        pairs.append((i, (((x * 2 + z_hi) * 4 + y) * 2 + z_lo) * 2 + core))
    return lax.ppermute(v, ("gx", "gy", "gz"), pairs)


def call(body, out_shape, in_specs, cost, out_specs=None, scratch=(), limit=56):
    if out_specs is None:
        out_specs = [VMEM] * len(out_shape)
    flops, moved = cost
    return pl.pallas_call(
        body,
        out_shape=[jax.ShapeDtypeStruct(*s) for s in out_shape],
        in_specs=in_specs,
        out_specs=out_specs,
        scratch_shapes=list(scratch),
        compiler_params=pltpu.CompilerParams(vmem_limit_bytes=limit * MIB),
        cost_estimate=pl.CostEstimate(flops=flops, bytes_accessed=moved, transcendentals=0),
    )


def one_hot(at=None):
    q = lax.broadcasted_iota(jnp.int32, (256, 256), 0)
    u = lax.broadcasted_iota(jnp.int32, (256, 256), 1)
    s = q // 32
    if at is not None:
        s = ((at[0] - s // 2) & 3) * 2 + ((at[1] + s) & 1)
    return jnp.where(u == (q % 32) * 8 + s, 1.0, 0.0).astype(bf16)


def group(at, k, z):
    return ((at[0] - k) & 3) * 2 + (at[1] ^ z)


def token_rows(y, k):
    return pl.ds(pl.multiple_of(((y - k) & 3) * 64, 64), 64)


def pack_body(at, pre, *outs):
    slope, parts = outs[0], outs[1:]
    pick = one_hot(at)
    for j in range(pre.shape[1] // 256):
        cols = slice(256 * j, 256 * j + 256)
        u = jnp.concatenate([pre[token_rows(at[2], k), cols] for k in range(4)], 0)
        u = u.astype(f32)
        t = jnp.tanh(tanh_scale * (u + cubic_coef * u * u * u))
        slope[:, cols] = 0.5 * (1.0 + t) + 0.5 * u * (1.0 - t * t) * tanh_scale * (
            1.0 + 3.0 * cubic_coef * u * u
        )
        hidden = (0.5 * u * (1.0 + t)).astype(bf16)
        turned = lax.dot_general(pick, hidden, (((1,), (1,)), ((), ())), preferred_element_type=f32)
        turned = turned.astype(bf16)
        for i in range(8):
            parts[i // 2][i % 2, 32 * j : 32 * j + 32, :] = turned[32 * i : 32 * i + 32, :]


def load_grads(at, pieces, held, sems):
    p0, p1, p3, p2p, p2m = pieces
    todo = [(p0, 0, 0), (p0, 0, 1), (p1, 1, 0), (p1, 1, 1), (p3, 3, 0), (p3, 3, 1), (p2p, 2, 0), (p2m, 2, 1)]

    def copies(core):
        made = []
        for n, (src, k, z) in enumerate(todo):
            src = src.at[z if src.shape[0] == 2 else 0]
            dst = held.at[k, z] if core == 0 else held.at[:, z, k]
            made.append(pltpu.make_async_copy(src, dst, sems.at[n]))
        return made

    for core in range(2):

        @pl.when(at[4] == core)
        def _():
            for c in copies(core):
                c.start()
            for c in copies(core):
                c.wait()


def input_body(count, at, w_hbm, *refs):
    pieces, (mine, theirs, w, held, sums, w_sem, in_sems, out_sems) = refs[:count], refs[count:]
    load = pltpu.make_async_copy(w_hbm, w, w_sem)
    load.start()
    blocks = [p.at[z] for p in pieces for z in range(p.shape[0])]
    for i, src in enumerate(blocks):
        pltpu.make_async_copy(src, held.at[i], in_sems.at[i]).start()
    load.wait()
    rows = w.shape[0] // 4

    def leaving(i):
        slot = i % 2
        return [
            pltpu.make_async_copy(sums.at[slot, at[4] ^ n], out.at[i], out_sems.at[slot, n])
            for n, out in enumerate((mine, theirs))
        ]

    @pl.loop(0, len(blocks))
    def _(i):
        pltpu.make_async_copy(blocks[0], held.at[i], in_sems.at[i]).wait()

        @pl.when(i >= 2)
        def _():
            for c in leaving(i - 2):
                c.wait()

        part = lax.dot_general(
            w[...], held[i].reshape(256, -1), (((1,), (1,)), ((), ())), preferred_element_type=f32
        ).astype(bf16)
        for n in range(4):
            sums[i % 2, n % 2, n // 2] = part[n * rows : n * rows + rows]
        for c in leaving(i):
            c.start()

    for i in range(len(blocks) - 2, len(blocks)):
        for c in leaving(i):
            c.wait()


def core_sum_body(at, mine, mine2, other, other2, out, given, held, in_sems, out_sems):
    def coming(n, z, k):
        early, late = ((mine, mine2), (other, other2))[n]
        src = late.at[z] if k == 2 else early.at[2 * (k - k // 3) + z]
        return pltpu.make_async_copy(src, given.at[n, z, k], in_sems.at[n, z, k])

    def leaving(z, k):
        return pltpu.make_async_copy(held.at[z, k], out.at[group(at, k, z)], out_sems.at[z, k])

    every = [(n, k) for n in range(2) for k in range(4)]
    for z in range(2):
        for n, k in every:
            coming(n, z, k).start()
    by_x, by_y = at[4], 1 - at[4]
    for z in range(2):
        for n, k in every:
            coming(n, z, k).wait()
        for k in range(4):
            lanes = pl.ds(64 * k, 64)
            for lo in range(2):
                turned = jnp.concatenate([given[by_y, z, n, lo, :, lanes] for n in range(4)], 1)
                held[z, k, lo] = (given[by_x, z, k, lo].astype(f32) + turned.astype(f32)).astype(bf16)
            leaving(z, k).start()
    for z in range(2):
        for k in range(4):
            leaving(z, k).wait()


def finish_body(at, slope, parts, out, held, sems):
    count = out.shape[1] // 256
    copies = [
        pltpu.make_async_copy(parts.at[:, :, pl.ds(32 * j, 32), :], held.at[j], sems.at[j]) for j in range(count)
    ]
    for c in copies:
        c.start()
    pick = one_hot()
    for j in range(count):
        cols = slice(256 * j, 256 * j + 256)
        copies[j].wait()
        v = [held[j, n, 0].astype(f32) + held[j, n, 1].astype(f32) for n in range(8)]
        v = jnp.concatenate(v, 0).astype(bf16)
        total = lax.dot_general(v, pick, (((0,), (0,)), ((), ())), preferred_element_type=f32)
        result = (total * slope[:, cols]).astype(bf16)
        for k in range(4):
            out[token_rows(at[2], k), cols] = result[64 * k : 64 * k + 64, :]


def weight_body(at, *refs):
    hidden, pieces, (out, held, sems) = refs[:4], refs[4:9], refs[9:]
    load_grads(at, pieces, held, sems)
    rows = out.shape[0] // 4
    lhs = jnp.concatenate(
        [jnp.concatenate([h[z, k] for k in range(4) for z in range(2)], 1) for h in hidden], 0
    )

    @pl.loop(0, out.shape[1] // 256)
    def _(j):
        cols = pl.ds(pl.multiple_of(j * 256, 256), 256)
        grads = held[:, :, :, :, cols].reshape(2048, 256)
        total = lax.dot_general(lhs, grads, (((1,), (0,)), ((), ())), preferred_element_type=f32)
        total = total.astype(bf16)
        for n, (lo, core) in enumerate(((0, 0), (1, 0), (0, 1), (1, 1))):
            block = ((at[3] + lo) & 1) * 2 + ((at[4] + core) & 1)
            out[pl.ds(pl.multiple_of(block * rows, 64), rows), cols] = total[n * rows : n * rows + rows]


def per_device(pre_act, grad_out, weight):
    tokens, columns = pre_act.shape
    rows, features = columns // 8, grad_out.shape[1]
    gx, y, gz = lax.axis_index("gx"), lax.axis_index("gy"), lax.axis_index("gz")
    at = jnp.stack([gx // 2, gx % 2, y, gz // 2, gz % 2]).astype(jnp.int32)
    w = weight.reshape(4 * rows, features)
    block = (rows, tokens)
    grad_scratch = [pltpu.VMEM((4, 2, 4, tokens // 4, features), bf16), pltpu.SemaphoreType.DMA((8,))]
    product = 2 * 4 * rows * 8 * tokens * features

    slope, *parts = call(
        pack_body,
        [((tokens, columns), f32)] + [((2,) + block, bf16)] * 4,
        [SMEM, VMEM],
        (2 * tokens * 256 * columns, 8 * tokens * columns),
    )(at, pre_act)

    other = swap_z_hi(grad_out)
    first = [[v] + [send_by_core(v, k, True) for k in (1, 2, 3)] for v in (grad_out, other)]

    by_x = [parts[0]] + [send_x(parts[4 - k], k) for k in (1, 2, 3)]
    first, by_x = lax.optimization_barrier((first, by_x))
    p0 = jnp.stack([jnp.stack(v) for v in first])
    p1, p3 = send_by_core(p0, 1, False), send_by_core(p0, 3, False)

    p2p, p2m = send_by_core(p1[:1], 1, False), send_by_core(p3[1:], 3, False)
    pieces = p0, p1, p3, p2p, p2m
    own = jnp.stack([p[0] for p in by_x])
    own = jnp.stack([own, swap_z_hi(jnp.stack([p[1] for p in by_x]))])
    far = swap_z_lo(own)

    def input_part(*given):
        count = sum(p.shape[0] for p in given)
        return call(
            functools.partial(input_body, len(given)),
            [((count, 2) + block, bf16)] * 2,
            [SMEM, HBM] + [HBM] * len(given),
            (product * count // 8, 2 * (4 * rows * features + count * (4 * rows + features) * tokens)),
            out_specs=[HBM] * 2,
            scratch=[
                pltpu.VMEM((4 * rows, features), bf16),
                pltpu.VMEM((count, 4, tokens // 4, features), bf16),
                pltpu.VMEM((2, 2, 2) + block, bf16),
                pltpu.SemaphoreType.DMA,
                pltpu.SemaphoreType.DMA((count,)),
                pltpu.SemaphoreType.DMA((2, 2)),
            ],
        )(at, w, *given)

    early = lax.optimization_barrier((p0, p1, p3, own))
    mine, theirs = input_part(*early[:3])
    other = swap_core(theirs)
    mine2, theirs2 = input_part(p2p, p2m)
    size = 2 * 4 * rows * tokens
    (sums,) = call(
        core_sum_body,
        [((8, 2) + block, bf16)],
        [SMEM] + [HBM] * 4,
        (4 * size, 12 * size),
        out_specs=[HBM],
        scratch=[
            pltpu.VMEM((2, 2, 4, 2) + block, bf16),
            pltpu.VMEM((2, 4, 2) + block, bf16),
            pltpu.SemaphoreType.DMA((2, 2, 4)),
            pltpu.SemaphoreType.DMA((2, 4)),
        ],
    )(at, mine, mine2, other, swap_core(theirs2))
    same_core = [[2 * (2 * i + k) + c for i in range(8) for k in range(2)] for c in range(2)]
    back = lax.all_to_all(
        sums.reshape((16,) + block), ("gx", "gz"), 0, 0, tiled=True, axis_index_groups=same_core
    )
    own, far, _ = lax.optimization_barrier((own, far, sums))
    hidden = [own, far, swap_core(own), swap_core(far)]
    (weight_grad,) = call(
        weight_body,
        [((4 * rows, features), bf16)],
        [SMEM] + [VMEM] * 4 + [HBM] * 5,
        (product, 2 * (8 * rows * features + 2048 * features)),
        scratch=grad_scratch,
    )(at, *hidden, *pieces)
    back, weight_grad = lax.optimization_barrier((back, weight_grad))
    (pre_grad,) = call(
        finish_body,
        [((tokens, columns), bf16)],
        [SMEM, VMEM, HBM],
        (2 * tokens * 256 * columns, 8 * tokens * columns),
        scratch=[pltpu.VMEM((6, 8, 2, 32, tokens), bf16), pltpu.SemaphoreType.DMA((6,))],
    )(at, slope, back.reshape((8, 2) + block))
    return pre_grad, weight_grad.reshape(weight.shape)


def solution(mesh):
    placed = (P("gx", ("gy", "gz")), P(("gx", "gy"), "gz"), P("gy", "gx", "gz"))
    return jax.shard_map(
        per_device,
        mesh=mesh,
        in_specs=placed,
        out_specs=(P("gx", ("gy", "gz")), P("gy", "gx", "gz")),
        check_vma=False,
    )
```

```python
import functools

import jax
import jax.numpy as jnp
from jax import lax
from jax.experimental import pallas as pl
from jax.experimental.pallas import tpu as pltpu
from jax.sharding import PartitionSpec as P

tanh_scale = 0.7978845608028654
cubic_coef = 0.044715
bf16 = jnp.bfloat16
f32 = jnp.float32
MIB = 1024 * 1024
VMEM = pl.BlockSpec(memory_space=pltpu.VMEM)
SMEM = pl.BlockSpec(memory_space=pltpu.SMEM)
ANY = pl.BlockSpec(memory_space=pl.ANY)


def send(v, axis, count, to):
    return lax.ppermute(v, axis, [(i, to(i)) for i in range(count)])


def send_x(v, d):
    return send(v, "gx", 8, lambda i: ((i // 2 + d) % 4) * 2 + i % 2)


def send_y(v, d):
    return send(v, "gy", 4, lambda i: (i + d) % 4)


def swap_z_hi(v):
    return send(v, "gx", 8, lambda i: i ^ 1)


def swap_z_lo(v):
    return send(v, "gz", 4, lambda i: i ^ 2)


def swap_core(v):
    return send(v, "gz", 4, lambda i: i ^ 1)


def send_by_core(v, d, first):
    pairs = []
    for i in range(128):
        x, z_hi, y, z_lo, core = i // 32, i // 16 % 2, i // 4 % 4, i // 2 % 2, i % 2
        if (core == 0) == first:
            y = (y + d) % 4
        else:
            x = (x + d) % 4
        pairs.append((i, (((x * 2 + z_hi) * 4 + y) * 2 + z_lo) * 2 + core))
    return lax.ppermute(v, ("gx", "gy", "gz"), pairs)


def call(body, out_shape, in_specs, cost, out_specs=None, scratch=(), limit=12):
    if out_specs is None:
        out_specs = [VMEM] * len(out_shape)
    flops, moved = cost
    return pl.pallas_call(
        body,
        out_shape=[jax.ShapeDtypeStruct(*s) for s in out_shape],
        in_specs=in_specs,
        out_specs=out_specs,
        scratch_shapes=list(scratch),
        compiler_params=pltpu.CompilerParams(vmem_limit_bytes=limit * MIB),
        cost_estimate=pl.CostEstimate(flops=flops, bytes_accessed=moved, transcendentals=0),
    )


def one_hot(at=None):
    q = lax.broadcasted_iota(jnp.int32, (256, 256), 0)
    u = lax.broadcasted_iota(jnp.int32, (256, 256), 1)
    s = q // 32
    if at is not None:
        s = ((at[0] - s // 2) & 3) * 2 + ((at[1] + s) & 1)
    return jnp.where(u == (q % 32) * 8 + s, 1.0, 0.0).astype(bf16)


def group(at, k, z):
    return ((at[0] - k) & 3) * 2 + (at[1] ^ z)


def token_rows(y, k):
    return pl.ds(pl.multiple_of(((y - k) & 3) * 64, 64), 64)


def pack_body(at, pre, *outs):
    slope, parts = outs[0], outs[1:]
    pick = one_hot(at)
    for j in range(pre.shape[1] // 256):
        cols = slice(256 * j, 256 * j + 256)
        u = jnp.concatenate([pre[token_rows(at[2], k), cols] for k in range(4)], 0)
        u = u.astype(f32)
        t = jnp.tanh(tanh_scale * (u + cubic_coef * u * u * u))
        slope[:, cols] = 0.5 * (1.0 + t) + 0.5 * u * (1.0 - t * t) * tanh_scale * (
            1.0 + 3.0 * cubic_coef * u * u
        )
        hidden = (0.5 * u * (1.0 + t)).astype(bf16)
        turned = lax.dot_general(pick, hidden, (((1,), (1,)), ((), ())), preferred_element_type=f32)
        turned = turned.astype(bf16)
        for i in range(8):
            parts[i // 2][i % 2, 32 * j : 32 * j + 32, :] = turned[32 * i : 32 * i + 32, :]


def load_grads(at, pieces, held, sems):
    p0, p1, p3, p2p, p2m = pieces
    todo = [(p0, 0, 0), (p0, 0, 1), (p1, 1, 0), (p1, 1, 1), (p3, 3, 0), (p3, 3, 1), (p2p, 2, 0), (p2m, 2, 1)]

    def copies(core):
        made = []
        for n, (src, k, z) in enumerate(todo):
            src = src.at[z if src.shape[0] == 2 else 0]
            dst = held.at[k, z] if core == 0 else held.at[:, z, k]
            made.append(pltpu.make_async_copy(src, dst, sems.at[n]))
        return made

    for core in range(2):

        @pl.when(at[4] == core)
        def _():
            for c in copies(core):
                c.start()
            for c in copies(core):
                c.wait()


def input_body(count, at, w_hbm, *refs):
    pieces, (mine, theirs, w, held, sums, w_sem, in_sems, out_sems) = refs[:count], refs[count:]
    load = pltpu.make_async_copy(w_hbm, w, w_sem)
    load.start()
    blocks = [p.at[z] for p in pieces for z in range(p.shape[0])]
    for i, src in enumerate(blocks):
        pltpu.make_async_copy(src, held.at[i], in_sems.at[i]).start()
    load.wait()
    rows = w.shape[0] // 4

    def leaving(i):
        slot = i % 2
        return [
            pltpu.make_async_copy(sums.at[slot, at[4] ^ n], out.at[i], out_sems.at[slot, n])
            for n, out in enumerate((mine, theirs))
        ]

    @pl.loop(0, len(blocks))
    def _(i):
        pltpu.make_async_copy(blocks[0], held.at[i], in_sems.at[i]).wait()

        @pl.when(i >= 2)
        def _():
            for c in leaving(i - 2):
                c.wait()

        part = lax.dot_general(
            w[...], held[i].reshape(256, -1), (((1,), (1,)), ((), ())), preferred_element_type=f32
        ).astype(bf16)
        for n in range(4):
            sums[i % 2, n % 2, n // 2] = part[n * rows : n * rows + rows]
        for c in leaving(i):
            c.start()

    for i in range(len(blocks) - 2, len(blocks)):
        for c in leaving(i):
            c.wait()


def core_sum_body(at, mine, mine2, other, other2, out, held, sems):
    def leaving(k, z):
        n = 2 * k + z
        return pltpu.make_async_copy(held.at[n], out.at[group(at, k, z)], sems.at[n])

    def block(early, late, k, z, lo, lanes=slice(None)):
        if k == 2:
            return late[z, lo, :, lanes]
        return early[2 * (k - k // 3) + z, lo, :, lanes]

    for core in range(2):

        @pl.when(at[4] == core)
        def _():
            by_x, by_y = (mine, mine2), (other, other2)
            if core:
                by_x, by_y = by_y, by_x
            for z in range(2):
                for lo in range(2):
                    for k in range(4):
                        lanes = pl.ds(64 * k, 64)
                        turned = jnp.concatenate([block(*by_y, n, z, lo, lanes) for n in range(4)], 1)
                        total = block(*by_x, k, z, lo).astype(f32) + turned.astype(f32)
                        held[2 * k + z, lo] = total.astype(bf16)
                for k in range(4):
                    leaving(k, z).start()

    for z in range(2):
        for k in range(4):
            leaving(k, z).wait()


def finish_body(at, slope, parts, out):
    pick = one_hot()
    for j in range(out.shape[1] // 256):
        cols, units = slice(256 * j, 256 * j + 256), slice(32 * j, 32 * j + 32)
        v = [(parts[n, 0, units, :].astype(f32) + parts[n, 1, units, :].astype(f32)) for n in range(8)]
        v = jnp.concatenate(v, 0).astype(bf16)
        total = lax.dot_general(v, pick, (((0,), (0,)), ((), ())), preferred_element_type=f32)
        result = (total * slope[:, cols]).astype(bf16)
        for k in range(4):
            out[token_rows(at[2], k), cols] = result[64 * k : 64 * k + 64, :]


def weight_body(at, *refs):
    hidden, pieces, (out, held, sems) = refs[:4], refs[4:9], refs[9:]
    load_grads(at, pieces, held, sems)
    rows = out.shape[0] // 4
    lhs = jnp.concatenate(
        [jnp.concatenate([h[z, k] for k in range(4) for z in range(2)], 1) for h in hidden], 0
    )

    @pl.loop(0, out.shape[1] // 256)
    def _(j):
        cols = pl.ds(pl.multiple_of(j * 256, 256), 256)
        grads = held[:, :, :, :, cols].reshape(2048, 256)
        total = lax.dot_general(lhs, grads, (((1,), (0,)), ((), ())), preferred_element_type=f32)
        total = total.astype(bf16)
        for n, (lo, core) in enumerate(((0, 0), (1, 0), (0, 1), (1, 1))):
            block = ((at[3] + lo) & 1) * 2 + ((at[4] + core) & 1)
            out[pl.ds(pl.multiple_of(block * rows, 64), rows), cols] = total[n * rows : n * rows + rows]


def per_device(pre_act, grad_out, weight):
    tokens, columns = pre_act.shape
    rows, features = columns // 8, grad_out.shape[1]
    gx, y, gz = lax.axis_index("gx"), lax.axis_index("gy"), lax.axis_index("gz")
    at = jnp.stack([gx // 2, gx % 2, y, gz // 2, gz % 2]).astype(jnp.int32)
    w = weight.reshape(4 * rows, features)
    block = (rows, tokens)
    grad_scratch = [pltpu.VMEM((4, 2, 4, tokens // 4, features), bf16), pltpu.SemaphoreType.DMA((8,))]
    product = 2 * 4 * rows * 8 * tokens * features

    slope, *parts = call(
        pack_body,
        [((tokens, columns), f32)] + [((2,) + block, bf16)] * 4,
        [SMEM, VMEM],
        (2 * tokens * 256 * columns, 8 * tokens * columns),
    )(at, pre_act)

    other = swap_z_hi(grad_out)
    first = [[v] + [send_by_core(v, k, True) for k in (1, 2, 3)] for v in (grad_out, other)]

    by_x = [parts[0]] + [send_x(parts[4 - k], k) for k in (1, 2, 3)]
    first, by_x = lax.optimization_barrier((first, by_x))
    p0 = jnp.stack([jnp.stack(v) for v in first])
    p1, p3 = send_by_core(p0, 1, False), send_by_core(p0, 3, False)

    p2p, p2m = send_by_core(p1[:1], 1, False), send_by_core(p3[1:], 3, False)
    pieces = p0, p1, p3, p2p, p2m
    own = jnp.stack([p[0] for p in by_x])
    own = jnp.stack([own, swap_z_hi(jnp.stack([p[1] for p in by_x]))])
    far = swap_z_lo(own)

    def input_part(*given):
        count = sum(p.shape[0] for p in given)
        return call(
            functools.partial(input_body, len(given)),
            [((count, 2) + block, bf16)] * 2,
            [SMEM, ANY] + [ANY] * len(given),
            (product * count // 8, 2 * (4 * rows * features + count * (4 * rows + features) * tokens)),
            out_specs=[ANY] * 2,
            scratch=[
                pltpu.VMEM((4 * rows, features), bf16),
                pltpu.VMEM((count, 4, tokens // 4, features), bf16),
                pltpu.VMEM((2, 2, 2) + block, bf16),
                pltpu.SemaphoreType.DMA,
                pltpu.SemaphoreType.DMA((count,)),
                pltpu.SemaphoreType.DMA((2, 2)),
            ],
            limit=10 + 2 * count,
        )(at, w, *given)

    early = lax.optimization_barrier((p0, p1, p3, own))
    mine, theirs = input_part(*early[:3])
    other = swap_core(theirs)
    mine2, theirs2 = input_part(p2p, p2m)
    size = 2 * 4 * rows * tokens
    (sums,) = call(
        core_sum_body,
        [((8, 2) + block, bf16)],
        [SMEM] + [VMEM] * 4,
        (4 * size, 12 * size),
        out_specs=[ANY],
        scratch=[pltpu.VMEM((8, 2) + block, bf16), pltpu.SemaphoreType.DMA((8,))],
        limit=12,
    )(at, mine, mine2, other, swap_core(theirs2))
    same_core = [[2 * (2 * i + k) + c for i in range(8) for k in range(2)] for c in range(2)]
    back = lax.all_to_all(
        sums.reshape((16,) + block), ("gx", "gz"), 0, 0, tiled=True, axis_index_groups=same_core
    )
    own, far, _ = lax.optimization_barrier((own, far, sums))
    hidden = [own, far, swap_core(own), swap_core(far)]
    (weight_grad,) = call(
        weight_body,
        [((4 * rows, features), bf16)],
        [SMEM] + [VMEM] * 4 + [ANY] * 5,
        (product, 2 * (8 * rows * features + 2048 * features)),
        scratch=grad_scratch,
        limit=32,
    )(at, *hidden, *pieces)
    back, weight_grad = lax.optimization_barrier((back, weight_grad))
    (pre_grad,) = call(
        finish_body,
        [((tokens, columns), bf16)],
        [SMEM] + [VMEM] * 2,
        (2 * tokens * 256 * columns, 8 * tokens * columns),
        limit=12,
    )(at, slope, back.reshape((8, 2) + block))
    return pre_grad, weight_grad.reshape(weight.shape)


def solution(mesh):
    placed = (P("gx", ("gy", "gz")), P(("gx", "gy"), "gz"), P("gy", "gx", "gz"))
    return jax.shard_map(
        per_device,
        mesh=mesh,
        in_specs=placed,
        out_specs=(P("gx", ("gy", "gz")), P("gy", "gx", "gz")),
        check_vma=False,
    )
```

```python
import functools

import jax
import jax.numpy as jnp
from jax import lax
from jax.experimental import pallas as pl
from jax.experimental.pallas import tpu as pltpu
from jax.sharding import PartitionSpec as P

tanh_scale = 0.7978845608028654
cubic_coef = 0.044715
bf16 = jnp.bfloat16
f32 = jnp.float32
MIB = 1024 * 1024
VMEM = pl.BlockSpec(memory_space=pltpu.VMEM)
SMEM = pl.BlockSpec(memory_space=pltpu.SMEM)
ANY = pl.BlockSpec(memory_space=pl.ANY)


def send(v, axis, count, to):
    return lax.ppermute(v, axis, [(i, to(i)) for i in range(count)])


def send_x(v, d):
    return send(v, "gx", 8, lambda i: ((i // 2 + d) % 4) * 2 + i % 2)


def send_y(v, d):
    return send(v, "gy", 4, lambda i: (i + d) % 4)


def swap_z_hi(v):
    return send(v, "gx", 8, lambda i: i ^ 1)


def swap_z_lo(v):
    return send(v, "gz", 4, lambda i: i ^ 2)


def swap_core(v):
    return send(v, "gz", 4, lambda i: i ^ 1)


def send_by_core(v, d, first):
    pairs = []
    for i in range(128):
        x, z_hi, y, z_lo, core = i // 32, i // 16 % 2, i // 4 % 4, i // 2 % 2, i % 2
        if (core == 0) == first:
            y = (y + d) % 4
        else:
            x = (x + d) % 4
        pairs.append((i, (((x * 2 + z_hi) * 4 + y) * 2 + z_lo) * 2 + core))
    return lax.ppermute(v, ("gx", "gy", "gz"), pairs)


def call(body, out_shape, in_specs, cost, out_specs=None, scratch=(), limit=12):
    if out_specs is None:
        out_specs = [VMEM] * len(out_shape)
    flops, moved = cost
    return pl.pallas_call(
        body,
        out_shape=[jax.ShapeDtypeStruct(*s) for s in out_shape],
        in_specs=in_specs,
        out_specs=out_specs,
        scratch_shapes=list(scratch),
        compiler_params=pltpu.CompilerParams(vmem_limit_bytes=limit * MIB),
        cost_estimate=pl.CostEstimate(flops=flops, bytes_accessed=moved, transcendentals=0),
    )


def one_hot(at=None):
    q = lax.broadcasted_iota(jnp.int32, (256, 256), 0)
    u = lax.broadcasted_iota(jnp.int32, (256, 256), 1)
    s = q // 32
    if at is not None:
        s = ((at[0] - s // 2) & 3) * 2 + ((at[1] + s) & 1)
    return jnp.where(u == (q % 32) * 8 + s, 1.0, 0.0).astype(bf16)


def group(at, k, z):
    return ((at[0] - k) & 3) * 2 + (at[1] ^ z)


def token_rows(y, k):
    return pl.ds(pl.multiple_of(((y - k) & 3) * 64, 64), 64)


def pack_body(at, pre, *outs):
    slope, parts = outs[0], outs[1:]
    pick = one_hot(at)
    for j in range(pre.shape[1] // 256):
        cols = slice(256 * j, 256 * j + 256)
        u = jnp.concatenate([pre[token_rows(at[2], k), cols] for k in range(4)], 0)
        u = u.astype(f32)
        t = jnp.tanh(tanh_scale * (u + cubic_coef * u * u * u))
        slope[:, cols] = 0.5 * (1.0 + t) + 0.5 * u * (1.0 - t * t) * tanh_scale * (
            1.0 + 3.0 * cubic_coef * u * u
        )
        hidden = (0.5 * u * (1.0 + t)).astype(bf16)
        turned = lax.dot_general(pick, hidden, (((1,), (1,)), ((), ())), preferred_element_type=f32)
        turned = turned.astype(bf16)
        for i in range(8):
            parts[i // 2][i % 2, 32 * j : 32 * j + 32, :] = turned[32 * i : 32 * i + 32, :]


def load_grads(at, pieces, held, sems):
    p0, p1, p3, p2p, p2m = pieces
    todo = [(p0, 0, 0), (p0, 0, 1), (p1, 1, 0), (p1, 1, 1), (p3, 3, 0), (p3, 3, 1), (p2p, 2, 0), (p2m, 2, 1)]

    def copies(core):
        made = []
        for n, (src, k, z) in enumerate(todo):
            src = src.at[z if src.shape[0] == 2 else 0]
            dst = held.at[k, z] if core == 0 else held.at[:, z, k]
            made.append(pltpu.make_async_copy(src, dst, sems.at[n]))
        return made

    for core in range(2):

        @pl.when(at[4] == core)
        def _():
            for c in copies(core):
                c.start()
            for c in copies(core):
                c.wait()


def input_body(count, at, w_hbm, *refs):
    pieces, (mine, theirs, w, held, sums, w_sem, in_sems, out_sems) = refs[:count], refs[count:]
    load = pltpu.make_async_copy(w_hbm, w, w_sem)
    load.start()
    blocks = [p.at[z] for p in pieces for z in range(p.shape[0])]
    for i, src in enumerate(blocks):
        pltpu.make_async_copy(src, held.at[i], in_sems.at[i]).start()
    load.wait()
    rows = w.shape[0] // 4

    def leaving(i):
        slot = i % 2
        return [
            pltpu.make_async_copy(sums.at[slot, at[4] ^ n], out.at[i], out_sems.at[slot, n])
            for n, out in enumerate((mine, theirs))
        ]

    @pl.loop(0, len(blocks))
    def _(i):
        pltpu.make_async_copy(blocks[0], held.at[i], in_sems.at[i]).wait()

        @pl.when(i >= 2)
        def _():
            for c in leaving(i - 2):
                c.wait()

        part = lax.dot_general(
            w[...], held[i].reshape(256, -1), (((1,), (1,)), ((), ())), preferred_element_type=f32
        ).astype(bf16)
        for n in range(4):
            sums[i % 2, n % 2, n // 2] = part[n * rows : n * rows + rows]
        for c in leaving(i):
            c.start()

    for i in range(len(blocks) - 2, len(blocks)):
        for c in leaving(i):
            c.wait()


def core_sum_body(at, mine, mine2, other, other2, out, held, sems):
    def leaving(k, z):
        n = 2 * k + z
        return pltpu.make_async_copy(held.at[n], out.at[group(at, k, z)], sems.at[n])

    def block(early, late, k, z, lo, lanes=slice(None)):
        if k == 2:
            return late[z, lo, :, lanes]
        return early[2 * (k - k // 3) + z, lo, :, lanes]

    for core in range(2):

        @pl.when(at[4] == core)
        def _():
            by_x, by_y = (mine, mine2), (other, other2)
            if core:
                by_x, by_y = by_y, by_x
            for z in range(2):
                for lo in range(2):
                    for k in range(4):
                        lanes = pl.ds(64 * k, 64)
                        turned = jnp.concatenate([block(*by_y, n, z, lo, lanes) for n in range(4)], 1)
                        total = block(*by_x, k, z, lo).astype(f32) + turned.astype(f32)
                        held[2 * k + z, lo] = total.astype(bf16)
                for k in range(4):
                    leaving(k, z).start()

    for z in range(2):
        for k in range(4):
            leaving(k, z).wait()


def finish_body(at, slope, parts, out):
    pick = one_hot()
    for j in range(out.shape[1] // 256):
        cols, units = slice(256 * j, 256 * j + 256), slice(32 * j, 32 * j + 32)
        v = [(parts[n, 0, units, :].astype(f32) + parts[n, 1, units, :].astype(f32)) for n in range(8)]
        v = jnp.concatenate(v, 0).astype(bf16)
        total = lax.dot_general(v, pick, (((0,), (0,)), ((), ())), preferred_element_type=f32)
        result = (total * slope[:, cols]).astype(bf16)
        for k in range(4):
            out[token_rows(at[2], k), cols] = result[64 * k : 64 * k + 64, :]


def weight_body(at, *refs):
    hidden, pieces, (out, held, own, sems, own_sems) = refs[:8], refs[8:13], refs[13:]
    copies = [pltpu.make_async_copy(h, own.at[n], own_sems.at[n]) for n, h in enumerate(hidden)]
    for c in copies:
        c.start()
    load_grads(at, pieces, held, sems)
    for c in copies:
        c.wait()
    rows = out.shape[0] // 4
    lhs = jnp.concatenate(
        [jnp.concatenate([own[2 * n + z, k] for k in range(4) for z in range(2)], 1) for n in range(4)], 0
    )

    @pl.loop(0, out.shape[1] // 256)
    def _(j):
        cols = pl.ds(pl.multiple_of(j * 256, 256), 256)
        grads = held[:, :, :, :, cols].reshape(2048, 256)
        total = lax.dot_general(lhs, grads, (((1,), (0,)), ((), ())), preferred_element_type=f32)
        total = total.astype(bf16)
        for n, (lo, core) in enumerate(((0, 0), (1, 0), (0, 1), (1, 1))):
            block = ((at[3] + lo) & 1) * 2 + ((at[4] + core) & 1)
            out[pl.ds(pl.multiple_of(block * rows, 64), rows), cols] = total[n * rows : n * rows + rows]


def per_device(pre_act, grad_out, weight):
    tokens, columns = pre_act.shape
    rows, features = columns // 8, grad_out.shape[1]
    gx, y, gz = lax.axis_index("gx"), lax.axis_index("gy"), lax.axis_index("gz")
    at = jnp.stack([gx // 2, gx % 2, y, gz // 2, gz % 2]).astype(jnp.int32)
    w = weight.reshape(4 * rows, features)
    block = (rows, tokens)
    product = 2 * 4 * rows * 8 * tokens * features

    slope, *parts = call(
        pack_body,
        [((tokens, columns), f32)] + [((2,) + block, bf16)] * 4,
        [SMEM, VMEM],
        (2 * tokens * 256 * columns, 8 * tokens * columns),
    )(at, pre_act)

    other = swap_z_hi(grad_out)
    first = [[v] + [send_by_core(v, k, True) for k in (1, 2, 3)] for v in (grad_out, other)]

    by_x = [parts[0]] + [send_x(parts[4 - k], k) for k in (1, 2, 3)]
    first, by_x = lax.optimization_barrier((first, by_x))
    p0 = jnp.stack([jnp.stack(v) for v in first])
    p1, p3 = send_by_core(p0, 1, False), send_by_core(p0, 3, False)

    p2p, p2m = send_by_core(p1[:1], 1, False), send_by_core(p3[1:], 3, False)
    pieces = p0, p1, p3, p2p, p2m
    own = [jnp.stack([p[0] for p in by_x]), swap_z_hi(jnp.stack([p[1] for p in by_x]))]
    far = [swap_z_lo(own[0])]

    def input_part(*given):
        count = sum(p.shape[0] for p in given)
        return call(
            functools.partial(input_body, len(given)),
            [((count, 2) + block, bf16)] * 2,
            [SMEM, ANY] + [ANY] * len(given),
            (product * count // 8, 2 * (4 * rows * features + count * (4 * rows + features) * tokens)),
            out_specs=[ANY] * 2,
            scratch=[
                pltpu.VMEM((4 * rows, features), bf16),
                pltpu.VMEM((count, 4, tokens // 4, features), bf16),
                pltpu.VMEM((2, 2, 2) + block, bf16),
                pltpu.SemaphoreType.DMA,
                pltpu.SemaphoreType.DMA((count,)),
                pltpu.SemaphoreType.DMA((2, 2)),
            ],
            limit=10 + 2 * count,
        )(at, w, *given)

    early = lax.optimization_barrier((p0, p1, p3, far[0], own[1]))
    far, own[1] = [early[3], swap_z_lo(early[4])], early[4]
    mine, theirs = input_part(*early[:3])
    other = swap_core(theirs)
    mine2, theirs2 = input_part(p2p, p2m)
    size = 2 * 4 * rows * tokens
    (sums,) = call(
        core_sum_body,
        [((8, 2) + block, bf16)],
        [SMEM] + [VMEM] * 4,
        (4 * size, 12 * size),
        out_specs=[ANY],
        scratch=[pltpu.VMEM((8, 2) + block, bf16), pltpu.SemaphoreType.DMA((8,))],
        limit=12,
    )(at, mine, mine2, other, swap_core(theirs2))
    same_core = [[2 * (2 * i + k) + c for i in range(8) for k in range(2)] for c in range(2)]
    back = lax.all_to_all(
        sums.reshape((16,) + block), ("gx", "gz"), 0, 0, tiled=True, axis_index_groups=same_core
    )
    near, _ = lax.optimization_barrier((own + far, sums))
    hidden = near + [swap_core(v) for v in near]
    (weight_grad,) = call(
        weight_body,
        [((4 * rows, features), bf16)],
        [SMEM] + [ANY] * 13,
        (product, 2 * (8 * rows * features + 2048 * features)),
        scratch=[
            pltpu.VMEM((4, 2, 4, tokens // 4, features), bf16),
            pltpu.VMEM((8, 4) + block, bf16),
            pltpu.SemaphoreType.DMA((8,)),
            pltpu.SemaphoreType.DMA((8,)),
        ],
        limit=24,
    )(at, *hidden, *pieces)
    back, weight_grad = lax.optimization_barrier((back, weight_grad))
    (pre_grad,) = call(
        finish_body,
        [((tokens, columns), bf16)],
        [SMEM] + [VMEM] * 2,
        (2 * tokens * 256 * columns, 8 * tokens * columns),
        limit=12,
    )(at, slope, back.reshape((8, 2) + block))
    return pre_grad, weight_grad.reshape(weight.shape)


def solution(mesh):
    placed = (P("gx", ("gy", "gz")), P(("gx", "gy"), "gz"), P("gy", "gx", "gz"))
    return jax.shard_map(
        per_device,
        mesh=mesh,
        in_specs=placed,
        out_specs=(P("gx", ("gy", "gz")), P("gy", "gx", "gz")),
        check_vma=False,
    )
```

```python
import functools

import jax
import jax.numpy as jnp
from jax import lax
from jax.experimental import pallas as pl
from jax.experimental.pallas import tpu as pltpu
from jax.sharding import PartitionSpec as P

tanh_scale = 0.7978845608028654
cubic_coef = 0.044715
bf16 = jnp.bfloat16
f32 = jnp.float32
MIB = 1024 * 1024
VMEM = pl.BlockSpec(memory_space=pltpu.VMEM)
SMEM = pl.BlockSpec(memory_space=pltpu.SMEM)
ANY = pl.BlockSpec(memory_space=pl.ANY)
HBM = pl.BlockSpec(memory_space=pltpu.HBM)


def send(v, axis, count, to):
    return lax.ppermute(v, axis, [(i, to(i)) for i in range(count)])


def send_x(v, d):
    return send(v, "gx", 8, lambda i: ((i // 2 + d) % 4) * 2 + i % 2)


def send_y(v, d):
    return send(v, "gy", 4, lambda i: (i + d) % 4)


def swap_z_hi(v):
    return send(v, "gx", 8, lambda i: i ^ 1)


def swap_z_lo(v):
    return send(v, "gz", 4, lambda i: i ^ 2)


def swap_core(v):
    return send(v, "gz", 4, lambda i: i ^ 1)


def send_by_core(v, d, first):
    pairs = []
    for i in range(128):
        x, z_hi, y, z_lo, core = i // 32, i // 16 % 2, i // 4 % 4, i // 2 % 2, i % 2
        if (core == 0) == first:
            y = (y + d) % 4
        else:
            x = (x + d) % 4
        pairs.append((i, (((x * 2 + z_hi) * 4 + y) * 2 + z_lo) * 2 + core))
    return lax.ppermute(v, ("gx", "gy", "gz"), pairs)


def call(body, out_shape, in_specs, cost, out_specs=None, scratch=(), limit=12):
    if out_specs is None:
        out_specs = [VMEM] * len(out_shape)
    flops, moved = cost
    return pl.pallas_call(
        body,
        out_shape=[jax.ShapeDtypeStruct(*s) for s in out_shape],
        in_specs=in_specs,
        out_specs=out_specs,
        scratch_shapes=list(scratch),
        compiler_params=pltpu.CompilerParams(vmem_limit_bytes=limit * MIB),
        cost_estimate=pl.CostEstimate(flops=flops, bytes_accessed=moved, transcendentals=0),
    )


def one_hot(at=None):
    q = lax.broadcasted_iota(jnp.int32, (256, 256), 0)
    u = lax.broadcasted_iota(jnp.int32, (256, 256), 1)
    s = q // 32
    if at is not None:
        s = ((at[0] - s // 2) & 3) * 2 + ((at[1] + s) & 1)
    return jnp.where(u == (q % 32) * 8 + s, 1.0, 0.0).astype(bf16)


def group(at, k, z):
    return ((at[0] - k) & 3) * 2 + (at[1] ^ z)


def token_rows(y, k):
    return pl.ds(pl.multiple_of(((y - k) & 3) * 64, 64), 64)


def pack_body(at, pre, *outs):
    slope, parts = outs[0], outs[1:]
    pick = one_hot(at)
    for j in range(pre.shape[1] // 256):
        cols = slice(256 * j, 256 * j + 256)
        u = jnp.concatenate([pre[token_rows(at[2], k), cols] for k in range(4)], 0)
        u = u.astype(f32)
        t = jnp.tanh(tanh_scale * (u + cubic_coef * u * u * u))
        slope[:, cols] = 0.5 * (1.0 + t) + 0.5 * u * (1.0 - t * t) * tanh_scale * (
            1.0 + 3.0 * cubic_coef * u * u
        )
        hidden = (0.5 * u * (1.0 + t)).astype(bf16)
        turned = lax.dot_general(pick, hidden, (((1,), (1,)), ((), ())), preferred_element_type=f32)
        turned = turned.astype(bf16)
        for i in range(8):
            parts[i // 2][i % 2, 32 * j : 32 * j + 32, :] = turned[32 * i : 32 * i + 32, :]


def load_grads(at, pieces, held, sems):
    p0, p1, p3, p2p, p2m = pieces
    todo = [(p0, 0, 0), (p0, 0, 1), (p1, 1, 0), (p1, 1, 1), (p3, 3, 0), (p3, 3, 1), (p2p, 2, 0), (p2m, 2, 1)]

    def copies(core):
        made = []
        for n, (src, k, z) in enumerate(todo):
            src = src.at[z if src.shape[0] == 2 else 0]
            dst = held.at[k, z] if core == 0 else held.at[:, z, k]
            made.append(pltpu.make_async_copy(src, dst, sems.at[n]))
        return made

    for core in range(2):

        @pl.when(at[4] == core)
        def _():
            for c in copies(core):
                c.start()
            for c in copies(core):
                c.wait()


def input_body(count, at, w_hbm, *refs):
    pieces, (mine, theirs, w, held, sums, w_sem, in_sems, out_sems) = refs[:count], refs[count:]
    load = pltpu.make_async_copy(w_hbm, w, w_sem)
    load.start()
    blocks = [p.at[z] for p in pieces for z in range(p.shape[0])]
    for i, src in enumerate(blocks):
        pltpu.make_async_copy(src, held.at[i], in_sems.at[i]).start()
    load.wait()
    rows = w.shape[0] // 4

    def leaving(i):
        slot = i % 2
        return [
            pltpu.make_async_copy(sums.at[slot, at[4] ^ n], out.at[i], out_sems.at[slot, n])
            for n, out in enumerate((mine, theirs))
        ]

    @pl.loop(0, len(blocks))
    def _(i):
        pltpu.make_async_copy(blocks[0], held.at[i], in_sems.at[i]).wait()

        @pl.when(i >= 2)
        def _():
            for c in leaving(i - 2):
                c.wait()

        part = lax.dot_general(
            w[...], held[i].reshape(256, -1), (((1,), (1,)), ((), ())), preferred_element_type=f32
        ).astype(bf16)
        for n in range(4):
            sums[i % 2, n % 2, n // 2] = part[n * rows : n * rows + rows]
        for c in leaving(i):
            c.start()

    for i in range(len(blocks) - 2, len(blocks)):
        for c in leaving(i):
            c.wait()


def core_sum_body(at, mine, mine2, other, other2, out, held, sems):
    def leaving(k, z):
        n = 2 * k + z
        return pltpu.make_async_copy(held.at[n], out.at[group(at, k, z)], sems.at[n])

    def block(early, late, k, z, lo, lanes=slice(None)):
        if k == 2:
            return late[z, lo, :, lanes]
        return early[2 * (k - k // 3) + z, lo, :, lanes]

    for core in range(2):

        @pl.when(at[4] == core)
        def _():
            by_x, by_y = (mine, mine2), (other, other2)
            if core:
                by_x, by_y = by_y, by_x
            for z in range(2):
                for lo in range(2):
                    for k in range(4):
                        lanes = pl.ds(64 * k, 64)
                        turned = jnp.concatenate([block(*by_y, n, z, lo, lanes) for n in range(4)], 1)
                        total = block(*by_x, k, z, lo).astype(f32) + turned.astype(f32)
                        held[2 * k + z, lo] = total.astype(bf16)
                for k in range(4):
                    leaving(k, z).start()

    for z in range(2):
        for k in range(4):
            leaving(k, z).wait()


def finish_body(at, slope, parts, out, held, sems):
    count = out.shape[1] // 256
    copies = [
        pltpu.make_async_copy(slope.at[:, pl.ds(256 * j, 256)], held.at[j], sems.at[j]) for j in range(count)
    ]
    for c in copies:
        c.start()
    pick = one_hot()
    for j in range(count):
        cols, units = slice(256 * j, 256 * j + 256), slice(32 * j, 32 * j + 32)
        v = [(parts[n, 0, units, :].astype(f32) + parts[n, 1, units, :].astype(f32)) for n in range(8)]
        v = jnp.concatenate(v, 0).astype(bf16)
        total = lax.dot_general(v, pick, (((0,), (0,)), ((), ())), preferred_element_type=f32)
        copies[j].wait()
        result = (total * held[j]).astype(bf16)
        for k in range(4):
            out[token_rows(at[2], k), cols] = result[64 * k : 64 * k + 64, :]


def weight_body(at, *refs):
    hidden, pieces, (out, held, own, sems, own_sems) = refs[:8], refs[8:13], refs[13:]
    copies = [pltpu.make_async_copy(h, own.at[n], own_sems.at[n]) for n, h in enumerate(hidden)]
    for c in copies:
        c.start()
    load_grads(at, pieces, held, sems)
    for c in copies:
        c.wait()
    rows = out.shape[0] // 4
    lhs = jnp.concatenate(
        [jnp.concatenate([own[2 * n + z, k] for k in range(4) for z in range(2)], 1) for n in range(4)], 0
    )

    @pl.loop(0, out.shape[1] // 256)
    def _(j):
        cols = pl.ds(pl.multiple_of(j * 256, 256), 256)
        grads = held[:, :, :, :, cols].reshape(2048, 256)
        total = lax.dot_general(lhs, grads, (((1,), (0,)), ((), ())), preferred_element_type=f32)
        total = total.astype(bf16)
        for n, (lo, core) in enumerate(((0, 0), (1, 0), (0, 1), (1, 1))):
            block = ((at[3] + lo) & 1) * 2 + ((at[4] + core) & 1)
            out[pl.ds(pl.multiple_of(block * rows, 64), rows), cols] = total[n * rows : n * rows + rows]


def per_device(pre_act, grad_out, weight):
    tokens, columns = pre_act.shape
    rows, features = columns // 8, grad_out.shape[1]
    gx, y, gz = lax.axis_index("gx"), lax.axis_index("gy"), lax.axis_index("gz")
    at = jnp.stack([gx // 2, gx % 2, y, gz // 2, gz % 2]).astype(jnp.int32)
    w = weight.reshape(4 * rows, features)
    block = (rows, tokens)
    product = 2 * 4 * rows * 8 * tokens * features

    slope, *parts = call(
        pack_body,
        [((tokens, columns), f32)] + [((2,) + block, bf16)] * 4,
        [SMEM, VMEM],
        (2 * tokens * 256 * columns, 8 * tokens * columns),
    )(at, pre_act)

    other = swap_z_hi(grad_out)
    first = [[v] + [send_by_core(v, k, True) for k in (1, 2, 3)] for v in (grad_out, other)]

    by_x = [parts[0]] + [send_x(parts[4 - k], k) for k in (1, 2, 3)]
    first, by_x = lax.optimization_barrier((first, by_x))
    p0 = jnp.stack([jnp.stack(v) for v in first])
    p1, p3 = send_by_core(p0, 1, False), send_by_core(p0, 3, False)

    p2p, p2m = send_by_core(p1[:1], 1, False), send_by_core(p3[1:], 3, False)
    pieces = p0, p1, p3, p2p, p2m
    keep, away = [jnp.stack([p[z] for p in by_x]) for z in range(2)]
    near = [keep, swap_z_hi(away), swap_z_lo(keep), send(away, ("gx", "gz"), 32, lambda i: i ^ 6)]

    def input_part(*given):
        count = sum(p.shape[0] for p in given)
        return call(
            functools.partial(input_body, len(given)),
            [((count, 2) + block, bf16)] * 2,
            [SMEM, ANY] + [ANY] * len(given),
            (product * count // 8, 2 * (4 * rows * features + count * (4 * rows + features) * tokens)),
            out_specs=[ANY] * 2,
            scratch=[
                pltpu.VMEM((4 * rows, features), bf16),
                pltpu.VMEM((count, 4, tokens // 4, features), bf16),
                pltpu.VMEM((2, 2, 2) + block, bf16),
                pltpu.SemaphoreType.DMA,
                pltpu.SemaphoreType.DMA((count,)),
                pltpu.SemaphoreType.DMA((2, 2)),
            ],
            limit=10 + 2 * count,
        )(at, w, *given)

    early, near = lax.optimization_barrier(((p0, p1, p3), near))
    mine, theirs = input_part(*early)
    other = swap_core(theirs)
    mine2, theirs2 = input_part(p2p, p2m)
    size = 2 * 4 * rows * tokens
    (sums,) = call(
        core_sum_body,
        [((8, 2) + block, bf16)],
        [SMEM] + [VMEM] * 4,
        (4 * size, 12 * size),
        out_specs=[ANY],
        scratch=[pltpu.VMEM((8, 2) + block, bf16), pltpu.SemaphoreType.DMA((8,))],
        limit=12,
    )(at, mine, mine2, other, swap_core(theirs2))
    same_core = [[2 * (2 * i + k) + c for i in range(8) for k in range(2)] for c in range(2)]
    back = lax.all_to_all(
        sums.reshape((16,) + block), ("gx", "gz"), 0, 0, tiled=True, axis_index_groups=same_core
    )
    near, _ = lax.optimization_barrier((near, sums))
    hidden = near + [swap_core(v) for v in near]
    (weight_grad,) = call(
        weight_body,
        [((4 * rows, features), bf16)],
        [SMEM] + [HBM] * 13,
        (product, 2 * (8 * rows * features + 2048 * features)),
        scratch=[
            pltpu.VMEM((4, 2, 4, tokens // 4, features), bf16),
            pltpu.VMEM((8, 4) + block, bf16),
            pltpu.SemaphoreType.DMA((8,)),
            pltpu.SemaphoreType.DMA((8,)),
        ],
        limit=56,
    )(at, *hidden, *pieces)
    back, weight_grad = lax.optimization_barrier((back, weight_grad))
    (pre_grad,) = call(
        finish_body,
        [((tokens, columns), bf16)],
        [SMEM, HBM, VMEM],
        (2 * tokens * 256 * columns, 8 * tokens * columns),
        scratch=[pltpu.VMEM((columns // 256, tokens, 256), f32), pltpu.SemaphoreType.DMA((columns // 256,))],
        limit=12,
    )(at, slope, back.reshape((8, 2) + block))
    return pre_grad, weight_grad.reshape(weight.shape)


def solution(mesh):
    placed = (P("gx", ("gy", "gz")), P(("gx", "gy"), "gz"), P("gy", "gx", "gz"))
    return jax.shard_map(
        per_device,
        mesh=mesh,
        in_specs=placed,
        out_specs=(P("gx", ("gy", "gz")), P("gy", "gx", "gz")),
        check_vma=False,
    )
```

```python
import functools

import jax
import jax.numpy as jnp
from jax import lax
from jax.experimental import pallas as pl
from jax.experimental.pallas import tpu as pltpu
from jax.sharding import PartitionSpec as P

tanh_scale = 0.7978845608028654
cubic_coef = 0.044715
bf16 = jnp.bfloat16
f32 = jnp.float32
MIB = 1024 * 1024
VMEM = pl.BlockSpec(memory_space=pltpu.VMEM)
SMEM = pl.BlockSpec(memory_space=pltpu.SMEM)
ANY = pl.BlockSpec(memory_space=pl.ANY)
HBM = pl.BlockSpec(memory_space=pltpu.HBM)


def send(v, axis, count, to):
    return lax.ppermute(v, axis, [(i, to(i)) for i in range(count)])


def send_x(v, d):
    return send(v, "gx", 8, lambda i: ((i // 2 + d) % 4) * 2 + i % 2)


def send_y(v, d):
    return send(v, "gy", 4, lambda i: (i + d) % 4)


def swap_z_hi(v):
    return send(v, "gx", 8, lambda i: i ^ 1)


def swap_z_lo(v):
    return send(v, "gz", 4, lambda i: i ^ 2)


def swap_core(v):
    return send(v, "gz", 4, lambda i: i ^ 1)


def send_by_core(v, d, first):
    pairs = []
    for i in range(128):
        x, z_hi, y, z_lo, core = i // 32, i // 16 % 2, i // 4 % 4, i // 2 % 2, i % 2
        if (core == 0) == first:
            y = (y + d) % 4
        else:
            x = (x + d) % 4
        pairs.append((i, (((x * 2 + z_hi) * 4 + y) * 2 + z_lo) * 2 + core))
    return lax.ppermute(v, ("gx", "gy", "gz"), pairs)


def call(body, out_shape, in_specs, cost, out_specs=None, scratch=(), limit=12):
    if out_specs is None:
        out_specs = [VMEM] * len(out_shape)
    flops, moved = cost
    return pl.pallas_call(
        body,
        out_shape=[jax.ShapeDtypeStruct(*s) for s in out_shape],
        in_specs=in_specs,
        out_specs=out_specs,
        scratch_shapes=list(scratch),
        compiler_params=pltpu.CompilerParams(vmem_limit_bytes=limit * MIB),
        cost_estimate=pl.CostEstimate(flops=flops, bytes_accessed=moved, transcendentals=0),
    )


def one_hot(at=None):
    q = lax.broadcasted_iota(jnp.int32, (256, 256), 0)
    u = lax.broadcasted_iota(jnp.int32, (256, 256), 1)
    s = q // 32
    if at is not None:
        s = ((at[0] - s // 2) & 3) * 2 + ((at[1] + s) & 1)
    return jnp.where(u == (q % 32) * 8 + s, 1.0, 0.0).astype(bf16)


def group(at, k, z):
    return ((at[0] - k) & 3) * 2 + (at[1] ^ z)


def token_rows(y, k):
    return pl.ds(pl.multiple_of(((y - k) & 3) * 64, 64), 64)


def pack_body(at, pre, *outs):
    slope, parts = outs[0], outs[1:]
    pick = one_hot(at)
    for j in range(pre.shape[1] // 256):
        cols = slice(256 * j, 256 * j + 256)
        u = jnp.concatenate([pre[token_rows(at[2], k), cols] for k in range(4)], 0)
        u = u.astype(f32)
        t = jnp.tanh(tanh_scale * (u + cubic_coef * u * u * u))
        slope[:, cols] = 0.5 * (1.0 + t) + 0.5 * u * (1.0 - t * t) * tanh_scale * (
            1.0 + 3.0 * cubic_coef * u * u
        )
        hidden = (0.5 * u * (1.0 + t)).astype(bf16)
        turned = lax.dot_general(pick, hidden, (((1,), (1,)), ((), ())), preferred_element_type=f32)
        turned = turned.astype(bf16)
        for i in range(8):
            parts[i // 2][i % 2, 32 * j : 32 * j + 32, :] = turned[32 * i : 32 * i + 32, :]


def load_grads(at, pieces, held, sems):
    p0, p1, p3, p2p, p2m = pieces
    todo = [(p0, 0, 0), (p0, 0, 1), (p1, 1, 0), (p1, 1, 1), (p3, 3, 0), (p3, 3, 1), (p2p, 2, 0), (p2m, 2, 1)]

    def copies(core):
        made = []
        for n, (src, k, z) in enumerate(todo):
            src = src.at[z if src.shape[0] == 2 else 0]
            dst = held.at[k, z] if core == 0 else held.at[:, z, k]
            made.append(pltpu.make_async_copy(src, dst, sems.at[n]))
        return made

    for core in range(2):

        @pl.when(at[4] == core)
        def _():
            for c in copies(core):
                c.start()
            for c in copies(core):
                c.wait()


def input_body(count, at, w_hbm, *refs):
    pieces, (mine, theirs, w, held, sums, w_sem, in_sems, out_sems) = refs[:count], refs[count:]
    load = pltpu.make_async_copy(w_hbm, w, w_sem)
    load.start()
    blocks = [p.at[z] for p in pieces for z in range(p.shape[0])]
    for i, src in enumerate(blocks):
        pltpu.make_async_copy(src, held.at[i], in_sems.at[i]).start()
    load.wait()
    rows = w.shape[0] // 4

    def leaving(i):
        slot = i % 2
        return [
            pltpu.make_async_copy(sums.at[slot, at[4] ^ n], out.at[i], out_sems.at[slot, n])
            for n, out in enumerate((mine, theirs))
        ]

    @pl.loop(0, len(blocks))
    def _(i):
        pltpu.make_async_copy(blocks[0], held.at[i], in_sems.at[i]).wait()

        @pl.when(i >= 2)
        def _():
            for c in leaving(i - 2):
                c.wait()

        part = lax.dot_general(
            w[...], held[i].reshape(256, -1), (((1,), (1,)), ((), ())), preferred_element_type=f32
        ).astype(bf16)
        for n in range(4):
            sums[i % 2, n % 2, n // 2] = part[n * rows : n * rows + rows]
        for c in leaving(i):
            c.start()

    for i in range(len(blocks) - 2, len(blocks)):
        for c in leaving(i):
            c.wait()


def core_sum_body(at, mine, mine2, other, other2, out, held, sems):
    def leaving(k, z):
        n = 2 * k + z
        return pltpu.make_async_copy(held.at[n], out.at[group(at, k, z)], sems.at[n])

    def block(early, late, k, z, lo, lanes=slice(None)):
        if k == 2:
            return late[z, lo, :, lanes]
        return early[2 * (k - k // 3) + z, lo, :, lanes]

    for core in range(2):

        @pl.when(at[4] == core)
        def _():
            by_x, by_y = (mine, mine2), (other, other2)
            if core:
                by_x, by_y = by_y, by_x
            for z in range(2):
                for lo in range(2):
                    for k in range(4):
                        lanes = pl.ds(64 * k, 64)
                        turned = jnp.concatenate([block(*by_y, n, z, lo, lanes) for n in range(4)], 1)
                        total = block(*by_x, k, z, lo).astype(f32) + turned.astype(f32)
                        held[2 * k + z, lo] = total.astype(bf16)
                for k in range(4):
                    leaving(k, z).start()

    for z in range(2):
        for k in range(4):
            leaving(k, z).wait()


def finish_body(at, slope, parts, out, held, sems):
    count = out.shape[1] // 256
    copies = [
        pltpu.make_async_copy(slope.at[:, pl.ds(256 * j, 256)], held.at[j], sems.at[j]) for j in range(count)
    ]
    for c in copies:
        c.start()
    pick = one_hot()
    for j in range(count):
        cols, units = slice(256 * j, 256 * j + 256), slice(32 * j, 32 * j + 32)
        v = [(parts[n, 0, units, :].astype(f32) + parts[n, 1, units, :].astype(f32)) for n in range(8)]
        v = jnp.concatenate(v, 0).astype(bf16)
        total = lax.dot_general(v, pick, (((0,), (0,)), ((), ())), preferred_element_type=f32)
        copies[j].wait()
        result = (total * held[j]).astype(bf16)
        for k in range(4):
            out[token_rows(at[2], k), cols] = result[64 * k : 64 * k + 64, :]


def weight_body(at, *refs):
    hidden, pieces, (out, held, own, sems, own_sems) = refs[:8], refs[8:13], refs[13:]
    copies = [pltpu.make_async_copy(h, own.at[n], own_sems.at[n]) for n, h in enumerate(hidden)]
    for c in copies:
        c.start()
    load_grads(at, pieces, held, sems)
    for c in copies:
        c.wait()
    rows = out.shape[0] // 4
    lhs = jnp.concatenate(
        [jnp.concatenate([own[2 * n + z, k] for k in range(4) for z in range(2)], 1) for n in range(4)], 0
    )

    @pl.loop(0, out.shape[1] // 256)
    def _(j):
        cols = pl.ds(pl.multiple_of(j * 256, 256), 256)
        grads = held[:, :, :, :, cols].reshape(2048, 256)
        total = lax.dot_general(lhs, grads, (((1,), (0,)), ((), ())), preferred_element_type=f32)
        total = total.astype(bf16)
        for n, (lo, core) in enumerate(((0, 0), (1, 0), (0, 1), (1, 1))):
            block = ((at[3] + lo) & 1) * 2 + ((at[4] + core) & 1)
            out[pl.ds(pl.multiple_of(block * rows, 64), rows), cols] = total[n * rows : n * rows + rows]


def per_device(pre_act, grad_out, weight):
    tokens, columns = pre_act.shape
    rows, features = columns // 8, grad_out.shape[1]
    gx, y, gz = lax.axis_index("gx"), lax.axis_index("gy"), lax.axis_index("gz")
    at = jnp.stack([gx // 2, gx % 2, y, gz // 2, gz % 2]).astype(jnp.int32)
    w = weight.reshape(4 * rows, features)
    block = (rows, tokens)
    product = 2 * 4 * rows * 8 * tokens * features

    slope, *parts = call(
        pack_body,
        [((tokens, columns), f32)] + [((2,) + block, bf16)] * 4,
        [SMEM, VMEM],
        (2 * tokens * 256 * columns, 8 * tokens * columns),
    )(at, pre_act)

    grad_out, parts = lax.optimization_barrier((grad_out, parts))
    other = swap_z_hi(grad_out)
    first = [[v] + [send_by_core(v, k, True) for k in (1, 2, 3)] for v in (grad_out, other)]

    by_x = [parts[0]] + [send_x(parts[4 - k], k) for k in (1, 2, 3)]
    first, by_x = lax.optimization_barrier((first, by_x))
    p0 = jnp.stack([jnp.stack(v) for v in first])
    p1, p3 = send_by_core(p0, 1, False), send_by_core(p0, 3, False)

    p2p, p2m = send_by_core(p1[:1], 1, False), send_by_core(p3[1:], 3, False)
    pieces = p0, p1, p3, p2p, p2m
    keep, away = [jnp.stack([p[z] for p in by_x]) for z in range(2)]
    near = [keep, swap_z_hi(away), swap_z_lo(keep), send(away, ("gx", "gz"), 32, lambda i: i ^ 6)]

    def input_part(*given):
        count = sum(p.shape[0] for p in given)
        return call(
            functools.partial(input_body, len(given)),
            [((count, 2) + block, bf16)] * 2,
            [SMEM, ANY] + [ANY] * len(given),
            (product * count // 8, 2 * (4 * rows * features + count * (4 * rows + features) * tokens)),
            out_specs=[ANY] * 2,
            scratch=[
                pltpu.VMEM((4 * rows, features), bf16),
                pltpu.VMEM((count, 4, tokens // 4, features), bf16),
                pltpu.VMEM((2, 2, 2) + block, bf16),
                pltpu.SemaphoreType.DMA,
                pltpu.SemaphoreType.DMA((count,)),
                pltpu.SemaphoreType.DMA((2, 2)),
            ],
            limit=10 + 2 * count,
        )(at, w, *given)

    early, near = lax.optimization_barrier(((p0, p1, p3), near))
    mine, theirs = input_part(*early)
    other = swap_core(theirs)
    mine2, theirs2 = input_part(p2p, p2m)
    size = 2 * 4 * rows * tokens
    (sums,) = call(
        core_sum_body,
        [((8, 2) + block, bf16)],
        [SMEM] + [VMEM] * 4,
        (4 * size, 12 * size),
        out_specs=[ANY],
        scratch=[pltpu.VMEM((8, 2) + block, bf16), pltpu.SemaphoreType.DMA((8,))],
        limit=12,
    )(at, mine, mine2, other, swap_core(theirs2))
    same_core = [[2 * (2 * i + k) + c for i in range(8) for k in range(2)] for c in range(2)]
    back = lax.all_to_all(
        sums.reshape((16,) + block), ("gx", "gz"), 0, 0, tiled=True, axis_index_groups=same_core
    )
    near, _ = lax.optimization_barrier((near, sums))
    hidden = near + [swap_core(v) for v in near]
    (weight_grad,) = call(
        weight_body,
        [((4 * rows, features), bf16)],
        [SMEM] + [HBM] * 13,
        (product, 2 * (8 * rows * features + 2048 * features)),
        scratch=[
            pltpu.VMEM((4, 2, 4, tokens // 4, features), bf16),
            pltpu.VMEM((8, 4) + block, bf16),
            pltpu.SemaphoreType.DMA((8,)),
            pltpu.SemaphoreType.DMA((8,)),
        ],
        limit=56,
    )(at, *hidden, *pieces)
    back, weight_grad = lax.optimization_barrier((back, weight_grad))
    (pre_grad,) = call(
        finish_body,
        [((tokens, columns), bf16)],
        [SMEM, HBM, VMEM],
        (2 * tokens * 256 * columns, 8 * tokens * columns),
        scratch=[pltpu.VMEM((columns // 256, tokens, 256), f32), pltpu.SemaphoreType.DMA((columns // 256,))],
        limit=12,
    )(at, slope, back.reshape((8, 2) + block))
    return pre_grad, weight_grad.reshape(weight.shape)


def solution(mesh):
    placed = (P("gx", ("gy", "gz")), P(("gx", "gy"), "gz"), P("gy", "gx", "gz"))
    return jax.shard_map(
        per_device,
        mesh=mesh,
        in_specs=placed,
        out_specs=(P("gx", ("gy", "gz")), P("gy", "gx", "gz")),
        check_vma=False,
    )
```
